32 devices in a mesh: ctx: 8 (over z, core), fsdp: 4 (over y, x).
Axes of the slice: x: 2, y: 2, z: 4, core: 2. Of those that a mesh axis runs over, the one named last changes fastest.
Arguments:
- tokens: bfloat16 [4, 1024, 2048], P('fsdp', 'ctx'), may hold values from -6 to 6
- block_order: int32 [8], replicated, may hold values from 0 to 7, each once
- norm_attn: bfloat16 [2048], P(('ctx', 'fsdp')), may hold values from 0.5 to 1.5
- w_query: bfloat16 [2048, 2048], P(('ctx', 'fsdp')), may hold values from -0.125 to 0.125
- w_key: bfloat16 [2048, 256], P(('ctx', 'fsdp')), may hold values from -0.125 to 0.125
- w_value: bfloat16 [2048, 256], P(('ctx', 'fsdp')), may hold values from -0.125 to 0.125
- w_out: bfloat16 [2048, 2048], P(('ctx', 'fsdp')), may hold values from -3 to 3
- norm_ffn: bfloat16 [2048], P(('ctx', 'fsdp')), may hold values from 0.5 to 1.5
- w_gate: bfloat16 [2048, 5632], P(('ctx', 'fsdp')), may hold values from -0.125 to 0.125
- w_up: bfloat16 [2048, 5632], P(('ctx', 'fsdp')), may hold values from -0.125 to 0.125
- w_down: bfloat16 [5632, 2048], P(('ctx', 'fsdp')), may hold values from -0.078125 to 0.078125
- cotangent: bfloat16 [4, 1024, 2048], P('fsdp', 'ctx'), may hold values from -6 to 6
Outputs:
- output: bfloat16 [4, 1024, 2048], P('fsdp', 'ctx')
- grad_tokens: bfloat16 [4, 1024, 2048], P('fsdp', 'ctx')
- grad_norm_attn: float32 [2048], P(('ctx', 'fsdp'))
- grad_query: float32 [2048, 2048], P(('ctx', 'fsdp'))
- grad_key: float32 [2048, 256], P(('ctx', 'fsdp'))
- grad_value: float32 [2048, 256], P(('ctx', 'fsdp'))
- grad_out: float32 [2048, 2048], P(('ctx', 'fsdp'))
- grad_norm_ffn: float32 [2048], P(('ctx', 'fsdp'))
- grad_gate: float32 [2048, 5632], P(('ctx', 'fsdp'))
- grad_up: float32 [2048, 5632], P(('ctx', 'fsdp'))
- grad_down: float32 [5632, 2048], P(('ctx', 'fsdp'))
The draws below stay inside these ranges and needn't reach their ends.
Inputs may be any that keep to these rules, and one draw needn't show every extreme that they name: Every value appears once; index c of ctx holds blocks block_order[c] and 2 * 8 - 1 - block_order[c] of every sequence it has.
All inputs are finite; a program needn't handle non-finite values.
Results may differ from the reference program's by a relative error of at most 0.014.
Values may be sent and summed in bfloat16 or wider, within the bound.
No kernel may reach another device: no remote copies, remote signals or barrier semaphores. Data moves between devices by JAX's collectives and lax.ppermute only.
A program may use at most 192 MiB of HBM per device.

```python
import math
import jax
import jax.numpy as jnp
from jax import lax

D = 2048
H = 32
KVH = 4
HD = 64
FF = 5632
TOK_DEV = 128
QW = 2048
KVW = 256
HALF = 64
LEN = 1024
SEQS = 4
N_CTX = 8


def level_of(key, shape, split, low, high):
    def one(position, shards_of):
        steps = jax.random.uniform(jax.random.fold_in(jax.random.fold_in(key, 6), position), (shards_of,), jnp.float32, low / len(split), high / len(split))
        return jnp.repeat(jnp.exp(steps), shape[position] // shards_of).reshape((-1,) + (1,) * (len(shape) - position - 1))

    loudness = one(*split[0])
    for cut in split[1:]:
        loudness = loudness * one(*cut)
    return loudness


def bell_draw(own_key, dims, spread, most, cuts=(), kind=jnp.bfloat16):
    factor_of = level_of(own_key, dims, cuts, -0.22, 0.18) if cuts else 1.0
    entries = jax.random.normal(own_key, dims, jnp.float32) * spread * factor_of
    return jnp.minimum(jnp.maximum(entries, -most), most).astype(kind)


def setup_inputs(seed: int = 0) -> dict:
    seeds = jax.random.split(jax.random.key(seed), 13)
    return {
        "tokens": bell_draw(seeds[0], (SEQS, LEN, D), 1.0, 6.0, ((0, 4), (1, 8))),
        "block_order": jax.random.permutation(seeds[1], N_CTX).astype(jnp.int32),
        "norm_attn": jnp.clip(1.0 + 0.1 * jax.random.normal(seeds[2], (D,), jnp.float32), 0.5, 1.5).astype(jnp.bfloat16),
        "w_query": bell_draw(seeds[3], (D, QW), D ** -0.5, 0.125, ((0, 32),)),
        "w_key": bell_draw(seeds[4], (D, KVW), D ** -0.5, 0.125, ((0, 32),)),
        "w_value": bell_draw(seeds[5], (D, KVW), D ** -0.5, 0.125, ((0, 32),)),
        "w_out": bell_draw(seeds[6], (QW, D), (max(1, 2 * QW // LEN)) ** -0.5, 3.0, ((0, 32),)),
        "norm_ffn": jnp.clip(1.0 + 0.1 * jax.random.normal(seeds[7], (D,), jnp.float32), 0.5, 1.5).astype(jnp.bfloat16),
        "w_gate": bell_draw(seeds[8], (D, FF), D ** -0.5, 0.125, ((0, 32),)),
        "w_up": bell_draw(seeds[9], (D, FF), D ** -0.5, 0.125, ((0, 32),)),
        "w_down": bell_draw(seeds[10], (FF, D), FF ** -0.5, 0.078125, ((0, 32),)),
        "cotangent": bell_draw(seeds[11], (SEQS, LEN, D), 1.0, 6.0, ((0, 4), (1, 8))),
    }


HIGH = lax.Precision.HIGHEST
EPS = 1e-05
THETA = 10000.0

@jax.custom_vjp
def low(v):
    return lax.optimization_barrier(v.astype(jnp.bfloat16)).astype(jnp.float32)

@jax.custom_vjp
def low_back(v):
    return v

def low_keep(v):
    return (low(v), None)

def low_pass(kept, grad):
    return (grad,)

def back_keep(v):
    return (v, None)

def back_low(kept, grad):
    return (low(grad),)
low.defvjp(low_keep, low_pass)
low_back.defvjp(back_keep, back_low)

def high_dot(left, right):
    return jnp.dot(left, right, precision=HIGH)

def rms_normed(values):
    return values * lax.rsqrt(lax.optimization_barrier(jnp.mean(values * values, axis=-1, keepdims=True)) + EPS)

def positions(block_order, row_count):
    row_ids = jnp.arange(row_count, dtype=jnp.int32)
    owner_index = row_ids // TOK_DEV
    within = row_ids % TOK_DEV
    paired = block_order[owner_index]
    block_id = jnp.where(within < HALF, paired, 2 * N_CTX - 1 - paired)
    return (block_id * HALF + within % HALF).astype(jnp.int32)

def rope_tables(pos):
    freqs = THETA ** (-(jnp.arange(HD // 2, dtype=jnp.float32) * 2.0 / HD))
    angles = pos.astype(jnp.float32)[:, None] * freqs[None, :]
    return (jnp.cos(angles)[:, None, :], jnp.sin(angles)[:, None, :])

def rotate(values, cos_table, sin_table):
    first_half = values[..., :HD // 2]
    second_half = values[..., HD // 2:]
    return jnp.concatenate([first_half * cos_table - second_half * sin_table, second_half * cos_table + first_half * sin_table], axis=-1)

def attend(queries, keys, values, pos):
    block_rows = math.gcd(LEN, 512)
    groups = H // KVH
    scale = HD ** (-0.5)
    q_blocks = queries.reshape(LEN // block_rows, block_rows, KVH, groups, HD)
    p_blocks = pos.reshape(LEN // block_rows, block_rows)
    key_heads = keys.reshape(LEN, KVH, HD)
    value_heads = values.reshape(LEN, KVH, HD)

    def one_block(pieces):
        q_part, p_part = pieces
        scores = jnp.einsum('qgjd,kgd->gjqk', q_part, key_heads, precision=HIGH) * scale
        scores = low_back(scores)
        visible = pos[None, :] <= p_part[:, None]
        scores = jnp.where(visible[None, None], scores, -jnp.inf)
        row_max = lax.optimization_barrier(jnp.max(scores, axis=-1, keepdims=True))
        exponent = jnp.exp(scores - row_max)
        probability = low(exponent / lax.optimization_barrier(jnp.sum(exponent, axis=-1, keepdims=True)))
        attended = jnp.einsum('gjqk,kgd->qgjd', probability, value_heads, precision=HIGH)
        return attended.reshape(block_rows, QW)
    return lax.map(jax.checkpoint(one_block), (q_blocks, p_blocks)).reshape(LEN, QW)

def layer(source, pos, gain_a, weight_q, weight_k, weight_v, weight_o, gain_f, weight_g, weight_u, weight_d):
    cos_table, sin_table = rope_tables(pos)
    hidden_a = low(rms_normed(source) * gain_a)
    queries = low(rotate(low_back(high_dot(hidden_a, weight_q)).reshape(LEN, H, HD), cos_table, sin_table).reshape(LEN, QW))
    keys = low(rotate(low_back(high_dot(hidden_a, weight_k)).reshape(LEN, KVH, HD), cos_table, sin_table).reshape(LEN, KVW))
    values = low(low_back(high_dot(hidden_a, weight_v)))
    attended = low(low_back(attend(queries, keys, values, pos)))
    residual = source + low_back(high_dot(attended, weight_o))
    hidden_f = low(rms_normed(residual) * gain_f)
    gate_pre = low_back(high_dot(hidden_f, weight_g))
    up_pre = low_back(high_dot(hidden_f, weight_u))
    gated_values = low(jax.nn.silu(gate_pre) * up_pre)
    return residual + low_back(high_dot(gated_values, weight_d))

def reference(tokens, block_order, norm_attn, w_query, w_key, w_value, w_out, norm_ffn, w_gate, w_up, w_down, cotangent):
    pos = positions(block_order, LEN)
    params = tuple((p.astype(jnp.float32) for p in (norm_attn, w_query, w_key, w_value, w_out, norm_ffn, w_gate, w_up, w_down)))

    def per_sequence(carry, item):
        sequence, cot_seq = item

        def forward(source, *weights):
            return layer(source, pos, *weights)
        result, pull = jax.vjp(forward, sequence.astype(jnp.float32), *params)
        grads = pull(cot_seq.astype(jnp.float32))
        updated = tuple((c + g for c, g in zip(carry, grads[1:])))
        return (updated, (result.astype(jnp.bfloat16), grads[0].astype(jnp.bfloat16)))
    start = tuple((jnp.zeros(p.shape, jnp.float32) for p in params))
    totals, (outputs, grads_in) = lax.scan(per_sequence, start, (tokens, cotangent))
    return (outputs, grads_in, totals[0], totals[1], totals[2], totals[3], totals[4], totals[5], totals[6], totals[7], totals[8])
```

```python
import jax
import jax.numpy as jnp
from jax import lax
from jax.sharding import PartitionSpec as P

H = 32
KVH = 4
HD = 64

EPS = 1e-05
THETA = 10000.0
BF = jnp.bfloat16
F32 = jnp.float32


def rms_parts(values):
    recip = lax.rsqrt(jnp.mean(values * values, axis=-1, keepdims=True) + EPS)
    return (values * recip, recip)


def norm_back(grad_in, normed, recip):
    return recip * (grad_in - normed * jnp.mean(grad_in * normed, axis=-1, keepdims=True))


def positions(block_order, row_count, tok_rows, ctx_count):
    row_ids = jnp.arange(row_count, dtype=jnp.int32)
    owner_index = row_ids // tok_rows
    within = row_ids % tok_rows
    half_rows = tok_rows // 2
    match = owner_index[:, None] == jnp.arange(ctx_count, dtype=jnp.int32)[None, :]
    paired = jnp.sum(jnp.where(match, block_order[None, :], 0), axis=1)
    block_id = jnp.where(within < half_rows, paired, 2 * ctx_count - 1 - paired)
    return block_id * half_rows + within % half_rows


def rope_tables(pos):
    freqs = THETA ** (-(jnp.arange(HD // 2, dtype=F32) * 2.0 / HD))
    angles = pos.astype(F32)[:, None] * freqs[None, :]
    return (jnp.cos(angles)[:, None, :], jnp.sin(angles)[:, None, :])


def rotate(values, cos_table, sin_table):
    first_half = values[..., : HD // 2]
    second_half = values[..., HD // 2 :]
    return jnp.concatenate(
        [
            first_half * cos_table - second_half * sin_table,
            second_half * cos_table + first_half * sin_table,
        ],
        axis=-1,
    )


def swap_f(value, step, f_count):
    return lax.ppermute(value, "fsdp", [(i, i ^ step) for i in range(f_count)])


def gather_f(value, f_index, f_count):
    out = jnp.zeros((f_count,) + value.shape, value.dtype)
    out = lax.dynamic_update_index_in_dim(out, value, f_index, 0)
    for step in range(1, f_count):
        out = lax.dynamic_update_index_in_dim(
            out, swap_f(value, step, f_count), f_index ^ step, 0
        )
    return out


def reduce_f(parts, f_index, f_count):
    total = lax.dynamic_index_in_dim(parts, f_index, 0, keepdims=False).astype(F32)
    low = parts.astype(BF)
    for step in range(1, f_count):
        piece = lax.dynamic_index_in_dim(low, f_index ^ step, 0, keepdims=False)
        total = total + swap_f(piece, step, f_count).astype(F32)
    return total


def dot(a, b):
    return jnp.dot(a, b, preferred_element_type=F32)


def dot_nt(a, b):
    return lax.dot_general(a, b, (((1,), (1,)), ((), ())), preferred_element_type=F32)


def dot_tn(a, b):
    return lax.dot_general(a, b, (((0,), (0,)), ((), ())), preferred_element_type=F32)


def on_device(
    tokens,
    block_order,
    norm_attn,
    w_query,
    w_key,
    w_value,
    w_out,
    norm_ffn,
    w_gate,
    w_up,
    w_down,
    cotangent,
):
    c_count = lax.axis_size("ctx")
    f_count = lax.axis_size("fsdp")
    f_index = lax.axis_index("fsdp")
    c_index = lax.axis_index("ctx")
    tok_rows = tokens.shape[1]
    width = tokens.shape[2]
    seq = tok_rows * c_count
    heads = H // c_count
    share = c_count // KVH
    q_cols = heads * HD
    rows = w_query.shape[0]
    ff_cols = w_gate.shape[1] // c_count
    scale = HD ** (-0.5)

    def to_columns(packed):
        moved = lax.all_to_all(packed, "ctx", split_axis=0, concat_axis=0, tiled=True)
        full = gather_f(moved, f_index, f_count)
        return full.transpose(1, 0, 2, 3).reshape(c_count * f_count * rows, packed.shape[2])

    def kv_pack(w):
        return jnp.repeat(w.reshape(rows, KVH, HD).transpose(1, 0, 2), share, axis=0)

    x_all = lax.all_gather(tokens[0], "ctx", axis=0, tiled=True)
    qkv_pack = jnp.concatenate(
        [
            w_query.reshape(rows, c_count, q_cols).transpose(1, 0, 2),
            kv_pack(w_key),
            kv_pack(w_value),
        ],
        axis=2,
    )
    w_qkv = to_columns(qkv_pack)
    gains = lax.all_gather(
        jnp.concatenate([norm_attn, norm_ffn])[None], ("ctx", "fsdp"), axis=0, tiled=True
    )
    gain_a = gains[:, :rows].reshape(width).astype(F32)
    gain_f = gains[:, rows:].reshape(width).astype(F32)
    w_o = gather_f(w_out, f_index, f_count).reshape(f_count * rows, width)
    gu_pack = jnp.concatenate(
        [
            w_gate.reshape(rows, c_count, ff_cols).transpose(1, 0, 2),
            w_up.reshape(rows, c_count, ff_cols).transpose(1, 0, 2),
        ],
        axis=2,
    )
    w_gu = to_columns(gu_pack)
    w_d = gather_f(w_down, f_index, f_count).reshape(ff_cols, width)
    g_all = lax.all_gather(cotangent[0], "ctx", axis=0, tiled=True)

    pos = positions(block_order, seq, tok_rows, c_count)
    cos_table, sin_table = rope_tables(pos)

    normed_all, _ = rms_parts(x_all.astype(F32))
    h1 = (normed_all * gain_a).astype(BF)
    qkv = dot(h1, w_qkv)
    q = rotate(qkv[:, :q_cols].reshape(seq, heads, HD), cos_table, sin_table).astype(BF)
    k = rotate(qkv[:, None, q_cols : q_cols + HD], cos_table, sin_table)[:, 0].astype(BF)
    v = qkv[:, q_cols + HD :].astype(BF)
    scores = jnp.einsum("qjd,kd->jqk", q, k, preferred_element_type=F32) * scale
    scores = jnp.where((pos[None, :] <= pos[:, None])[None], scores, -jnp.inf)
    row_max = jnp.max(scores, axis=-1, keepdims=True)
    exponent = jnp.exp(scores - row_max)
    prob = exponent / jnp.sum(exponent, axis=-1, keepdims=True)
    prob_low = prob.astype(BF)
    o = jnp.einsum("jqk,kd->qjd", prob_low, v, preferred_element_type=F32)
    o = o.astype(BF).reshape(seq, q_cols)
    y_rows = lax.psum_scatter(dot(o, w_o).astype(BF), "ctx", scatter_dimension=0, tiled=True)
    source = tokens[0].astype(F32)
    residual = source + y_rows.astype(F32)
    normed_f, recip_f = rms_parts(residual)
    h2 = lax.all_gather((normed_f * gain_f).astype(BF), "ctx", axis=0, tiled=True)

    gu = dot(h2, w_gu)
    gate = gu[:, :ff_cols]
    up = gu[:, ff_cols:]
    sig = jax.nn.sigmoid(gate)
    act = gate * sig
    z = (act * up).astype(BF)
    out_rows = lax.psum_scatter(dot(z, w_d).astype(BF), "ctx", scatter_dimension=0, tiled=True)
    result = (residual + out_rows.astype(F32)).astype(BF)
    dz = dot_nt(g_all, w_d)
    dub = (dz * act).astype(BF)
    dgb = (dz * up * sig * (1.0 + gate * (1.0 - sig))).astype(BF)
    dgu = jnp.concatenate([dgb, dub], axis=1)
    dh2 = lax.psum_scatter(dot_nt(dgu, w_gu).astype(BF), "ctx", scatter_dimension=0, tiled=True)
    dh2 = dh2.astype(F32)

    def from_columns(full):
        cols = full.shape[1]
        parts = full.reshape(c_count, f_count, rows, cols).transpose(1, 0, 2, 3)
        owned = reduce_f(parts, f_index, f_count)
        return lax.all_to_all(owned.astype(BF), "ctx", split_axis=0, concat_axis=0, tiled=True)

    grad_gu = from_columns(dot_tn(h2, dgu))
    shard_down = reduce_f(dot_tn(z, g_all).reshape(f_count, -1, width), f_index, f_count)
    shard_gate = grad_gu[:, :, :ff_cols].transpose(1, 0, 2).reshape(rows, -1).astype(F32)
    shard_up = grad_gu[:, :, ff_cols:].transpose(1, 0, 2).reshape(rows, -1).astype(F32)

    grad_gain_f = jnp.sum(dh2 * normed_f, axis=0)
    d_res = cotangent[0].astype(F32) + norm_back(dh2 * gain_f, normed_f, recip_f)
    ab = lax.all_gather(d_res.astype(BF), "ctx", axis=0, tiled=True)
    shard_out = reduce_f(dot_tn(o, ab).reshape(f_count, rows, width), f_index, f_count)
    d_o = dot_nt(ab, w_o).astype(BF).reshape(seq, heads, HD)
    d_prob = jnp.einsum("qjd,kd->jqk", d_o, v, preferred_element_type=F32)
    delta = jnp.sum(prob * d_prob, axis=-1, keepdims=True)
    d_s = (prob * (d_prob - delta)).astype(BF)
    dq = jnp.einsum("jqk,kd->qjd", d_s, k, preferred_element_type=F32) * scale
    dk = jnp.einsum("jqk,qjd->kd", d_s, q, preferred_element_type=F32) * scale
    dv = jnp.einsum("jqk,qjd->kd", prob_low, d_o, preferred_element_type=F32)
    dq = rotate(dq, cos_table, -sin_table).astype(BF).reshape(seq, q_cols)
    dk = rotate(dk[:, None], cos_table, -sin_table)[:, 0].astype(BF)
    dqkv = jnp.concatenate([dq, dk, dv.astype(BF)], axis=1)
    dh1_part = dot_nt(dqkv, w_qkv)
    dh1 = lax.psum_scatter(dh1_part.astype(BF), "ctx", scatter_dimension=0, tiled=True)
    dh1 = dh1.astype(F32)
    grad_qkv = from_columns(dot_tn(h1, dqkv))
    shard_query = grad_qkv[:, :, :q_cols].transpose(1, 0, 2).reshape(rows, -1).astype(F32)
    grad_kv = jnp.sum(
        grad_qkv[:, :, q_cols:].reshape(KVH, share, rows, 2 * HD).astype(F32), axis=1
    )
    shard_key = grad_kv[:, :, :HD].transpose(1, 0, 2).reshape(rows, -1)
    shard_value = grad_kv[:, :, HD:].transpose(1, 0, 2).reshape(rows, -1)

    normed_a, recip_a = rms_parts(source)
    grad_gain_a = jnp.sum(dh1 * normed_a, axis=0)
    grad_tokens = d_res + norm_back(dh1 * gain_a, normed_a, recip_a)
    shard_gain_a = lax.psum_scatter(grad_gain_a, ("ctx", "fsdp"), scatter_dimension=0, tiled=True)
    shard_gain_f = lax.psum_scatter(grad_gain_f, ("ctx", "fsdp"), scatter_dimension=0, tiled=True)
    return (
        result[None],
        grad_tokens.astype(BF)[None],
        shard_gain_a,
        shard_query,
        shard_key,
        shard_value,
        shard_out,
        shard_gain_f,
        shard_gate,
        shard_up,
        shard_down,
    )


def solution(mesh):
    both = ("ctx", "fsdp")
    row = P(both, None)
    in_specs = (
        P("fsdp", "ctx", None),
        P(),
        P(both),
        row,
        row,
        row,
        row,
        P(both),
        row,
        row,
        row,
        P("fsdp", "ctx", None),
    )
    out_specs = (
        P("fsdp", "ctx", None),
        P("fsdp", "ctx", None),
        P(both),
        row,
        row,
        row,
        row,
        P(both),
        row,
        row,
        row,
    )
    return jax.shard_map(
        on_device, mesh=mesh, in_specs=in_specs, out_specs=out_specs, check_vma=False
    )
```

```python
import functools

import jax
import jax.numpy as jnp
from jax import lax
from jax.experimental import pallas as pl
from jax.experimental.pallas import tpu as pltpu
from jax.sharding import PartitionSpec as P

H = 32
KVH = 4
HD = 64

EPS = 1e-05
THETA = 10000.0
BF = jnp.bfloat16
F32 = jnp.float32
FFN_ROWS = 256


def rms_parts(values):
    recip = lax.rsqrt(jnp.mean(values * values, axis=-1, keepdims=True) + EPS)
    return (values * recip, recip)


def norm_back(grad_in, normed, recip):
    return recip * (grad_in - normed * jnp.mean(grad_in * normed, axis=-1, keepdims=True))


def positions(block_order, row_count, tok_rows, ctx_count):
    row_ids = jnp.arange(row_count, dtype=jnp.int32)
    owner_index = row_ids // tok_rows
    within = row_ids % tok_rows
    half_rows = tok_rows // 2
    match = owner_index[:, None] == jnp.arange(ctx_count, dtype=jnp.int32)[None, :]
    paired = jnp.sum(jnp.where(match, block_order[None, :], 0), axis=1)
    block_id = jnp.where(within < half_rows, paired, 2 * ctx_count - 1 - paired)
    return block_id * half_rows + within % half_rows


def rope_tables(pos):
    freqs = THETA ** (-(jnp.arange(HD // 2, dtype=F32) * 2.0 / HD))
    angles = pos.astype(F32)[:, None] * freqs[None, :]
    return (jnp.cos(angles)[:, None, :], jnp.sin(angles)[:, None, :])


def turn(values):
    return jnp.concatenate([values[..., HD // 2 :], -values[..., : HD // 2]], axis=-1)


def rotate(values, cos_table, sin_table):
    first_half = values[..., : HD // 2]
    second_half = values[..., HD // 2 :]
    return jnp.concatenate(
        [
            first_half * cos_table - second_half * sin_table,
            second_half * cos_table + first_half * sin_table,
        ],
        axis=-1,
    )


def after(value, *others):
    return lax.optimization_barrier((value,) + others)[0]


def swap_f(value, step, f_count):
    return lax.ppermute(value, "fsdp", [(i, i ^ step) for i in range(f_count)])


def swap_core(value, c_count):
    return lax.ppermute(value, "ctx", [(i, i ^ 1) for i in range(c_count)])


def pick(stack, index, axis=0):
    return lax.dynamic_index_in_dim(stack, index, axis, keepdims=False)


def place_f(pieces, axis, f_index):
    value = pieces[0]
    shape = value.shape[:axis] + (len(pieces),) + value.shape[axis:]
    out = jnp.zeros(shape, value.dtype)
    for step, piece in enumerate(pieces):
        out = lax.dynamic_update_index_in_dim(out, piece, f_index ^ step, axis)
    return out


def fetch_f(value, f_count):
    return [value] + [swap_f(value, step, f_count) for step in range(1, f_count)]


def send_f(parts, axis, f_index, f_count):
    pieces = []
    for step in range(f_count):
        piece = pick(parts, f_index ^ step, axis)
        pieces.append(swap_f(piece, step, f_count) if step else piece)
    return pieces


def total_f(pieces, *others):
    return sum(after(piece, *others).astype(F32) for piece in pieces)


def gather_c(rows):
    return lax.all_gather(rows, "ctx", axis=0, tiled=True)


def scatter_c(full):
    return lax.psum_scatter(full, "ctx", scatter_dimension=0, tiled=True)


def exchange_z(blocks, c_count):
    groups = [list(range(core, c_count, 2)) for core in range(2)]
    return lax.all_to_all(
        blocks, "ctx", split_axis=0, concat_axis=0, tiled=True, axis_index_groups=groups
    )


def pair_sum(full, c_count):
    core = lax.axis_index("ctx") % 2
    parts = full.reshape(c_count // 2, 2, full.shape[0] // c_count, full.shape[1])
    got = swap_core(pick(parts, 1 - core, 1), c_count)
    return (pick(parts, core, 1).astype(F32) + got.astype(F32)).astype(BF)


def dot(a, b):
    return jnp.dot(a, b, preferred_element_type=F32)


def dot_nt(a, b):
    return lax.dot_general(a, b, (((1,), (1,)), ((), ())), preferred_element_type=F32)


def dot_tn(a, b):
    return lax.dot_general(a, b, (((0,), (0,)), ((), ())), preferred_element_type=F32)


def halves_of(value, half):
    rows, cols = value.shape
    blocks = value.reshape(rows // (2 * half), 2, half, cols)
    return [blocks[:, i].reshape(rows // 2, cols) for i in range(2)]


def merge_halves(first, second, half):
    rows, cols = first.shape
    blocks = [v.reshape(rows // half, 1, half, cols) for v in (first, second)]
    return jnp.concatenate(blocks, axis=1).reshape(2 * rows, cols)


def soft_parts(q_pair, k_pair, cols, rows_pos):
    scale = HD ** (-0.5)
    s_aa = jnp.where(rows_pos[0] <= cols[0], dot_nt(q_pair[0], k_pair[0]) * scale, -jnp.inf)
    s_ba = dot_nt(q_pair[1], k_pair[0]) * scale
    s_bb = jnp.where(rows_pos[1] <= cols[1], dot_nt(q_pair[1], k_pair[1]) * scale, -jnp.inf)
    m_a = jnp.max(s_aa, axis=1, keepdims=True)
    m_b = jnp.maximum(jnp.max(s_ba, axis=1, keepdims=True), jnp.max(s_bb, axis=1, keepdims=True))
    e_aa, e_ba, e_bb = jnp.exp(s_aa - m_a), jnp.exp(s_ba - m_b), jnp.exp(s_bb - m_b)
    r_a = 1.0 / jnp.sum(e_aa, axis=1, keepdims=True)
    r_b = 1.0 / (jnp.sum(e_ba, axis=1, keepdims=True) + jnp.sum(e_bb, axis=1, keepdims=True))
    return e_aa * r_a, e_ba * r_b, e_bb * r_b


def attend_kernel(half, q_ref, k_ref, v_ref, col_ref, row_ref, o_ref):
    cols = halves_of(col_ref[...], half)
    rows_pos = [row_ref[0:1], row_ref[1:2]]
    k_pair, v_pair = halves_of(k_ref[...], half), halves_of(v_ref[...], half)
    outs = []
    for j in range(q_ref.shape[1] // HD):
        q_pair = halves_of(q_ref[:, j * HD : (j + 1) * HD], half)
        p_aa, p_ba, p_bb = soft_parts(q_pair, k_pair, cols, rows_pos)
        o_a = dot(p_aa.astype(BF), v_pair[0])
        o_b = dot(p_ba.astype(BF), v_pair[0]) + dot(p_bb.astype(BF), v_pair[1])
        outs.append(merge_halves(o_a.astype(BF), o_b.astype(BF), half))
    o_ref[...] = jnp.concatenate(outs, axis=1)


def attend_back_kernel(half, q_ref, k_ref, v_ref, do_ref, kr_ref, qr_ref, cos_ref, sin_ref, col_ref, row_ref, dq_ref, dk_ref, dv_ref, acc_ref):
    scale = HD ** (-0.5)
    cols = halves_of(col_ref[...], half)
    rows_pos = [row_ref[0:1], row_ref[1:2]]
    k_pair, v_pair = halves_of(k_ref[...], half), halves_of(v_ref[...], half)
    kr_pair = halves_of(kr_ref[...], half)
    kk = [jnp.concatenate([k_pair[i], kr_pair[i]], axis=1) for i in range(2)]
    cos_pair, sin_pair = halves_of(cos_ref[...], half), halves_of(sin_ref[...], half)

    @pl.when(pl.program_id(0) == 0)
    def _():
        acc_ref[...] = jnp.zeros_like(acc_ref)

    dqs = []
    for j in range(q_ref.shape[1] // HD):
        lanes = slice(j * HD, (j + 1) * HD)
        q_pair = halves_of(q_ref[:, lanes], half)
        do_pair = halves_of(do_ref[:, lanes], half)
        qr_pair = halves_of(qr_ref[:, lanes], half)
        qq = [jnp.concatenate([q_pair[i], qr_pair[i]], axis=1) for i in range(2)]
        p_aa, p_ba, p_bb = soft_parts(q_pair, k_pair, cols, rows_pos)
        g_aa = dot_nt(do_pair[0], v_pair[0])
        g_ba = dot_nt(do_pair[1], v_pair[0])
        g_bb = dot_nt(do_pair[1], v_pair[1])
        d_a = jnp.sum(p_aa * g_aa, axis=1, keepdims=True)
        d_b = jnp.sum(p_ba * g_ba, axis=1, keepdims=True) + jnp.sum(p_bb * g_bb, axis=1, keepdims=True)
        s_aa = (p_aa * (g_aa - d_a)).astype(BF)
        s_ba = (p_ba * (g_ba - d_b)).astype(BF)
        s_bb = (p_bb * (g_bb - d_b)).astype(BF)
        dq_pair = [dot(s_aa, kk[0]), dot(s_ba, kk[0]) + dot(s_bb, kk[1])]
        out = []
        for i in range(2):
            d = dq_pair[i] * scale
            out.append((d[:, :HD] * cos_pair[i] + d[:, HD:] * sin_pair[i]).astype(BF))
        dqs.append(merge_halves(out[0], out[1], half))
        acc_ref[0, :, : 2 * HD] += dot_tn(s_aa, qq[0]) + dot_tn(s_ba, qq[1])
        acc_ref[1, :, : 2 * HD] += dot_tn(s_bb, qq[1])
        acc_ref[0, :, 2 * HD : 3 * HD] += dot_tn(p_aa.astype(BF), do_pair[0]) + dot_tn(p_ba.astype(BF), do_pair[1])
        acc_ref[1, :, 2 * HD : 3 * HD] += dot_tn(p_bb.astype(BF), do_pair[1])
    dq_ref[...] = jnp.concatenate(dqs, axis=1)

    @pl.when(pl.program_id(0) == pl.num_programs(0) - 1)
    def _():
        dk = []
        for i in range(2):
            d = acc_ref[i, :, : 2 * HD] * scale
            dk.append((d[:, :HD] * cos_pair[i] + d[:, HD:] * sin_pair[i]).astype(BF))
        dk_ref[...] = merge_halves(dk[0], dk[1], half)
        dv_ref[...] = merge_halves(acc_ref[0, :, 2 * HD : 3 * HD].astype(BF), acc_ref[1, :, 2 * HD : 3 * HD].astype(BF), half)


def whole(shape):
    return pl.BlockSpec(shape, lambda g: (0,) * len(shape))


def attend(q, k, v, col, row, half):
    seq, q_cols = q.shape
    by_pair = pl.BlockSpec((seq, 2 * HD), lambda g: (0, g))
    return pl.pallas_call(
        functools.partial(attend_kernel, half),
        grid=(q_cols // (2 * HD),),
        in_specs=[by_pair, whole(k.shape), whole(v.shape), whole(col.shape), whole(row.shape)],
        out_specs=by_pair,
        out_shape=jax.ShapeDtypeStruct((seq, q_cols), BF),
        compiler_params=pltpu.CompilerParams(vmem_limit_bytes=56 * 2**20),
    )(q, k, v, col, row)


def attend_back(q, k, v, do, kr, qr, cos, sin, col, row, half):
    seq, q_cols = q.shape
    by_pair = pl.BlockSpec((seq, 2 * HD), lambda g: (0, g))
    return pl.pallas_call(
        functools.partial(attend_back_kernel, half),
        grid=(q_cols // (2 * HD),),
        in_specs=[by_pair, whole(k.shape), whole(v.shape), by_pair, whole(kr.shape), by_pair, whole(cos.shape), whole(sin.shape), whole(col.shape), whole(row.shape)],
        out_specs=[by_pair, whole(k.shape), whole(v.shape)],
        out_shape=[jax.ShapeDtypeStruct((seq, q_cols), BF), jax.ShapeDtypeStruct(k.shape, BF), jax.ShapeDtypeStruct(v.shape, BF)],
        scratch_shapes=[pltpu.VMEM((2, seq // 2, 4 * HD), F32)],
        compiler_params=pltpu.CompilerParams(vmem_limit_bytes=56 * 2**20),
    )(q, k, v, do, kr, qr, cos, sin, col, row)


def ffn_kernel(h_ref, g_ref, wgu_ref, wd_ref, z_ref, dgu_ref, out_ref, dh_ref):
    ff = z_ref.shape[1]
    gu = dot(h_ref[...], wgu_ref[...])
    gate, up = gu[:, :ff], gu[:, ff:]
    sig = 1.0 / (1.0 + jnp.exp(-gate))
    act = gate * sig
    z = (act * up).astype(BF)
    z_ref[...] = z
    dz = dot_nt(g_ref[...], wd_ref[...])
    dub = (dz * act).astype(BF)
    dgb = (dz * up * (sig * (1.0 + gate * (1.0 - sig)))).astype(BF)
    dgu = jnp.concatenate([dgb, dub], axis=1)
    dgu_ref[...] = dgu
    dh_ref[...] = dot_nt(dgu, wgu_ref[...]).astype(BF)
    out_ref[...] = dot(z, wd_ref[...]).astype(BF)


def ffn(h, g, w_gu, w_d, block):
    seq, width = h.shape
    ff = w_d.shape[0]
    rows = pl.BlockSpec((block, width), lambda i: (i, 0))
    return pl.pallas_call(
        ffn_kernel,
        grid=(seq // block,),
        in_specs=[rows, rows, whole(w_gu.shape), whole(w_d.shape)],
        out_specs=[pl.BlockSpec((block, ff), lambda i: (i, 0)), pl.BlockSpec((block, 2 * ff), lambda i: (i, 0)), rows, rows],
        out_shape=[jax.ShapeDtypeStruct((seq, ff), BF), jax.ShapeDtypeStruct((seq, 2 * ff), BF), jax.ShapeDtypeStruct((seq, width), BF), jax.ShapeDtypeStruct((seq, width), BF)],
        compiler_params=pltpu.CompilerParams(vmem_limit_bytes=56 * 2**20),
    )(h, g, w_gu, w_d)


def on_device(
    tokens,
    block_order,
    norm_attn,
    w_query,
    w_key,
    w_value,
    w_out,
    norm_ffn,
    w_gate,
    w_up,
    w_down,
    cotangent,
):
    c_count = lax.axis_size("ctx")
    f_count = lax.axis_size("fsdp")
    f_index = lax.axis_index("fsdp")
    tok_rows = tokens.shape[1]
    width = tokens.shape[2]
    seq = tok_rows * c_count
    half = tok_rows // 2
    heads = H // c_count
    share = c_count // KVH
    q_cols = heads * HD
    a_cols = q_cols + 2 * HD
    rows = w_query.shape[0]
    ff_cols = w_gate.shape[1] // c_count

    def to_dest(packed):
        return lax.all_to_all(packed, "ctx", split_axis=0, concat_axis=0, tiled=True)

    def by_dest(w):
        return w.reshape(rows, c_count, -1).transpose(1, 0, 2)

    def kv_dest(w):
        return jnp.repeat(w.reshape(rows, KVH, HD).transpose(1, 0, 2), share, axis=0)

    pos = positions(block_order, seq, tok_rows, c_count)
    cos_table, sin_table = rope_tables(pos)
    cos_wide = jnp.concatenate([cos_table, cos_table], axis=2)[:, 0]
    sin_wide = jnp.concatenate([sin_table, sin_table], axis=2)[:, 0]
    pos_col = pos[:, None]
    pos_row = pos.reshape(c_count, 2, half).transpose(1, 0, 2).reshape(2, seq // 2)
    x_all = gather_c(tokens[0])
    gain_pack = jnp.pad(jnp.stack([norm_attn, norm_ffn], axis=1), ((0, 0), (0, 126)))
    qkv_pack = jnp.concatenate(
        [
            by_dest(w_query),
            kv_dest(w_key),
            kv_dest(w_value),
            jnp.broadcast_to(gain_pack[None], (c_count, rows, 128)),
        ],
        axis=2,
    )
    moved_qkv = to_dest(qkv_pack)
    d_pieces = fetch_f(w_down, f_count)
    w_qkvg = place_f(fetch_f(after(moved_qkv, *d_pieces), f_count), 1, f_index).reshape(width, a_cols + 128)
    w_qkv = w_qkvg[:, :a_cols]
    unit = jnp.eye(8, 128, dtype=BF)
    gains = dot_nt(unit, w_qkvg[:, a_cols:])
    gain_a = gains[0]
    gain_f = gains[1]
    w_o = place_f(fetch_f(w_out, f_count), 0, f_index).reshape(f_count * rows, width)
    moved_gu = to_dest(after(jnp.concatenate([by_dest(w_gate), by_dest(w_up)], axis=2), moved_qkv))
    gu_pieces = fetch_f(moved_gu, f_count)

    x_seen = after(x_all, w_qkvg, w_o, moved_gu, cos_wide, sin_wide, pos_col, pos_row)
    normed_all, _ = rms_parts(x_seen.astype(F32))
    h1 = (normed_all * gain_a).astype(BF)
    g_all = gather_c(after(cotangent[0], h1))
    qkv = dot(h1, w_qkv)
    q = rotate(qkv[:, :q_cols].reshape(seq, heads, HD), cos_table, sin_table).astype(BF)
    k = rotate(qkv[:, None, q_cols : q_cols + HD], cos_table, sin_table).astype(BF)
    q_turn = turn(q).reshape(seq, q_cols)
    k_turn = turn(k)[:, 0]
    q = q.reshape(seq, q_cols)
    k = k[:, 0]
    v = qkv[:, q_cols + HD :].astype(BF)
    o = attend(q, k, v, pos_col, pos_row, half)
    y_part = dot(o, w_o).astype(BF)
    y_rows = scatter_c(after(y_part, g_all, *gu_pieces[:3]))

    source = tokens[0].astype(F32)
    residual = source + y_rows.astype(F32)
    normed_f, recip_f = rms_parts(residual)
    w_d = place_f(d_pieces, 0, f_index).reshape(ff_cols, width)
    w_gu = place_f(gu_pieces, 1, f_index).reshape(width, 2 * ff_cols)
    h2_rows = after((normed_f * gain_f).astype(BF), w_gu, w_d)
    h2 = gather_c(h2_rows)

    z, dgu, out_part, dh2_part = ffn(h2, g_all, w_gu, w_d, FFN_ROWS)
    dh2 = scatter_c(dh2_part)
    grad_gu_low = dot_tn(after(h2, dh2_part), dgu).astype(BF)
    sent_gu = send_f(grad_gu_low.reshape(c_count, f_count, rows, -1), 1, f_index, f_count)
    grad_down_low = dot_tn(z, after(g_all, grad_gu_low)).astype(BF)
    sent_down = send_f(grad_down_low.reshape(f_count, -1, width), 0, f_index, f_count)
    out_mine = pair_sum(out_part, c_count)

    out_blocks = exchange_z(out_mine, c_count)
    d_h = after(dh2, grad_down_low, out_blocks, *sent_gu).astype(F32)
    gain_terms_f = jnp.sum(d_h * normed_f, axis=0)
    d_res = cotangent[0].astype(F32) + norm_back(d_h * gain_f, normed_f, recip_f)
    ab_rows = d_res.astype(BF)
    ab = gather_c(ab_rows)
    sum_gu = total_f(sent_gu, ab_rows).astype(BF)
    shard_down = total_f(sent_down, sum_gu)
    out_sum = jnp.sum(after(out_blocks, ab_rows).astype(F32), axis=0)
    result = (residual + out_sum).astype(BF)
    ab = after(ab, sum_gu, shard_down, result)

    d_o = dot_nt(ab, w_o).astype(BF)
    owned_gu = to_dest(after(sum_gu, d_o))
    dq, dk, dv = attend_back(
        q, k, v, d_o, k_turn, q_turn, cos_wide, sin_wide, pos_col, pos_row, half
    )
    dqkv = jnp.concatenate([dq, dk, dv], axis=1)
    dh1_part = dot_nt(dqkv, w_qkv)
    dh1_low = after(dh1_part.astype(BF), owned_gu)
    dh1 = scatter_c(dh1_low)
    gain_terms_a = jnp.sum(dh1_part * normed_all, axis=0)

    terms = jnp.stack([gain_terms_a, gain_terms_f])
    high = terms.astype(BF)
    low = (terms - high.astype(F32)).astype(BF)
    gain_cols = dot_tn(jnp.concatenate([high, low]), jnp.eye(4, 128, dtype=BF)).astype(BF)
    grad_qkv_low = jnp.concatenate([dot_tn(after(h1, dh1_low), dqkv).astype(BF), gain_cols], axis=1)
    sent_qkv = send_f(grad_qkv_low.reshape(c_count, f_count, rows, -1), 1, f_index, f_count)
    grad_out_low = dot_tn(after(o, grad_qkv_low), ab).astype(BF)
    sent_out = send_f(grad_out_low.reshape(f_count, rows, width), 0, f_index, f_count)
    owned_qkv = to_dest(total_f(sent_qkv, owned_gu).astype(BF))
    shard_out = total_f(sent_out)
    shard_gate = owned_gu[:, :, :ff_cols].transpose(1, 0, 2).reshape(rows, -1).astype(F32)
    shard_up = owned_gu[:, :, ff_cols:].transpose(1, 0, 2).reshape(rows, -1).astype(F32)
    shard_query = owned_qkv[:, :, :q_cols].transpose(1, 0, 2).reshape(rows, -1).astype(F32)
    grad_kv = jnp.sum(
        owned_qkv[:, :, q_cols:a_cols].reshape(KVH, share, rows, 2 * HD).astype(F32), axis=1
    )
    shard_key = grad_kv[:, :, :HD].transpose(1, 0, 2).reshape(rows, -1)
    shard_value = grad_kv[:, :, HD:].transpose(1, 0, 2).reshape(rows, -1)
    gain_sums = jnp.sum(owned_qkv[:, :, a_cols : a_cols + 4].astype(F32), axis=0)

    normed_a, recip_a = rms_parts(source)
    grads = d_res + norm_back(dh1.astype(F32) * gain_a, normed_a, recip_a)
    return (
        result[None],
        grads.astype(BF)[None],
        gain_sums[:, 0] + gain_sums[:, 2],
        shard_query,
        shard_key,
        shard_value,
        shard_out,
        gain_sums[:, 1] + gain_sums[:, 3],
        shard_gate,
        shard_up,
        shard_down,
    )


def solution(mesh):
    both = ("ctx", "fsdp")
    row = P(both, None)
    in_specs = (
        P("fsdp", "ctx", None),
        P(),
        P(both),
        row,
        row,
        row,
        row,
        P(both),
        row,
        row,
        row,
        P("fsdp", "ctx", None),
    )
    out_specs = (
        P("fsdp", "ctx", None),
        P("fsdp", "ctx", None),
        P(both),
        row,
        row,
        row,
        row,
        P(both),
        row,
        row,
        row,
    )
    return jax.shard_map(
        on_device, mesh=mesh, in_specs=in_specs, out_specs=out_specs, check_vma=False
    )
```

```python
import functools

import jax
import jax.numpy as jnp
from jax import lax
from jax.experimental import pallas as pl
from jax.experimental.pallas import tpu as pltpu
from jax.sharding import PartitionSpec as P

H = 32
KVH = 4
HD = 64

EPS = 1e-05
THETA = 10000.0
BF = jnp.bfloat16
F32 = jnp.float32
FFN_ROWS = 256
SUM_COST = 40 * 10**9


def rms_parts(values):
    recip = lax.rsqrt(jnp.mean(values * values, axis=-1, keepdims=True) + EPS)
    return (values * recip, recip)


def norm_back(grad_in, normed, recip):
    return recip * (grad_in - normed * jnp.mean(grad_in * normed, axis=-1, keepdims=True))


def positions(block_order, row_count, tok_rows, ctx_count):
    row_ids = jnp.arange(row_count, dtype=jnp.int32)
    owner_index = row_ids // tok_rows
    within = row_ids % tok_rows
    half_rows = tok_rows // 2
    match = owner_index[:, None] == jnp.arange(ctx_count, dtype=jnp.int32)[None, :]
    paired = jnp.sum(jnp.where(match, block_order[None, :], 0), axis=1)
    block_id = jnp.where(within < half_rows, paired, 2 * ctx_count - 1 - paired)
    return block_id * half_rows + within % half_rows


def rope_tables(pos):
    freqs = THETA ** (-(jnp.arange(HD // 2, dtype=F32) * 2.0 / HD))
    angles = pos.astype(F32)[:, None] * freqs[None, :]
    return (jnp.cos(angles)[:, None, :], jnp.sin(angles)[:, None, :])


def turn(values):
    return jnp.concatenate([values[..., HD // 2 :], -values[..., : HD // 2]], axis=-1)


def rotate(values, cos_table, sin_table):
    first_half = values[..., : HD // 2]
    second_half = values[..., HD // 2 :]
    return jnp.concatenate(
        [
            first_half * cos_table - second_half * sin_table,
            second_half * cos_table + first_half * sin_table,
        ],
        axis=-1,
    )


def after(value, *others):
    return lax.optimization_barrier((value,) + others)[0]


def swap_f(value, step, f_count):
    return lax.ppermute(value, "fsdp", [(i, i ^ step) for i in range(f_count)])


def swap_core(value, c_count):
    return lax.ppermute(value, "ctx", [(i, i ^ 1) for i in range(c_count)])


def pick(stack, index, axis=0):
    return lax.dynamic_index_in_dim(stack, index, axis, keepdims=False)


def place_f(pieces, axis, f_index):
    value = pieces[0]
    shape = value.shape[:axis] + (len(pieces),) + value.shape[axis:]
    out = jnp.zeros(shape, value.dtype)
    for step, piece in enumerate(pieces):
        out = lax.dynamic_update_index_in_dim(out, piece, f_index ^ step, axis)
    return out


def fetch_f(value, f_count):
    return [value] + [swap_f(value, step, f_count) for step in range(1, f_count)]


def send_f(parts, axis, f_index, f_count):
    pieces = []
    for step in range(f_count):
        piece = pick(parts, f_index ^ step, axis)
        pieces.append(swap_f(piece, step, f_count) if step else piece)
    return pieces


def total_f(pieces, *others):
    return sum(after(piece, *others).astype(F32) for piece in pieces)


def gather_c(rows):
    return lax.all_gather(rows, "ctx", axis=0, tiled=True)


def scatter_c(full):
    return lax.psum_scatter(full, "ctx", scatter_dimension=0, tiled=True)


def exchange_z(blocks, c_count):
    groups = [list(range(core, c_count, 2)) for core in range(2)]
    return lax.all_to_all(
        blocks, "ctx", split_axis=0, concat_axis=0, tiled=True, axis_index_groups=groups
    )


def pair_sum(full, c_count):
    core = lax.axis_index("ctx") % 2
    parts = full.reshape(c_count // 2, 2, full.shape[0] // c_count, full.shape[1])
    got = swap_core(pick(parts, 1 - core, 1), c_count)
    return (pick(parts, core, 1).astype(F32) + got.astype(F32)).astype(BF)


def dot(a, b):
    return jnp.dot(a, b, preferred_element_type=F32)


def dot_nt(a, b):
    return lax.dot_general(a, b, (((1,), (1,)), ((), ())), preferred_element_type=F32)


def dot_tn(a, b):
    return lax.dot_general(a, b, (((0,), (0,)), ((), ())), preferred_element_type=F32)


def halves_of(value, half):
    rows, cols = value.shape
    blocks = value.reshape(rows // (2 * half), 2, half, cols)
    return [blocks[:, i].reshape(rows // 2, cols) for i in range(2)]


def merge_halves(first, second, half):
    rows, cols = first.shape
    blocks = [v.reshape(rows // half, 1, half, cols) for v in (first, second)]
    return jnp.concatenate(blocks, axis=1).reshape(2 * rows, cols)


def soft_parts(q_pair, k_pair, cols, rows_pos):
    scale = HD ** (-0.5)
    s_aa = jnp.where(rows_pos[0] <= cols[0], dot_nt(q_pair[0], k_pair[0]) * scale, -jnp.inf)
    s_ba = dot_nt(q_pair[1], k_pair[0]) * scale
    s_bb = jnp.where(rows_pos[1] <= cols[1], dot_nt(q_pair[1], k_pair[1]) * scale, -jnp.inf)
    m_a = jnp.max(s_aa, axis=1, keepdims=True)
    m_b = jnp.maximum(jnp.max(s_ba, axis=1, keepdims=True), jnp.max(s_bb, axis=1, keepdims=True))
    e_aa, e_ba, e_bb = jnp.exp(s_aa - m_a), jnp.exp(s_ba - m_b), jnp.exp(s_bb - m_b)
    r_a = 1.0 / jnp.sum(e_aa, axis=1, keepdims=True)
    r_b = 1.0 / (jnp.sum(e_ba, axis=1, keepdims=True) + jnp.sum(e_bb, axis=1, keepdims=True))
    return e_aa * r_a, e_ba * r_b, e_bb * r_b


def attend_kernel(half, q_ref, k_ref, v_ref, col_ref, row_ref, o_ref):
    cols = halves_of(col_ref[...], half)
    rows_pos = [row_ref[0:1], row_ref[1:2]]
    k_pair, v_pair = halves_of(k_ref[...], half), halves_of(v_ref[...], half)
    outs = []
    for j in range(q_ref.shape[1] // HD):
        q_pair = halves_of(q_ref[:, j * HD : (j + 1) * HD], half)
        p_aa, p_ba, p_bb = soft_parts(q_pair, k_pair, cols, rows_pos)
        o_a = dot(p_aa.astype(BF), v_pair[0])
        o_b = dot(p_ba.astype(BF), v_pair[0]) + dot(p_bb.astype(BF), v_pair[1])
        outs.append(merge_halves(o_a.astype(BF), o_b.astype(BF), half))
    o_ref[...] = jnp.concatenate(outs, axis=1)


def attend_back_kernel(half, q_ref, k_ref, v_ref, do_ref, kr_ref, qr_ref, cos_ref, sin_ref, col_ref, row_ref, dq_ref, dk_ref, dv_ref, acc_ref):
    scale = HD ** (-0.5)
    cols = halves_of(col_ref[...], half)
    rows_pos = [row_ref[0:1], row_ref[1:2]]
    k_pair, v_pair = halves_of(k_ref[...], half), halves_of(v_ref[...], half)
    kr_pair = halves_of(kr_ref[...], half)
    kk = [jnp.concatenate([k_pair[i], kr_pair[i]], axis=1) for i in range(2)]
    cos_pair, sin_pair = halves_of(cos_ref[...], half), halves_of(sin_ref[...], half)

    @pl.when(pl.program_id(0) == 0)
    def _():
        acc_ref[...] = jnp.zeros_like(acc_ref)

    dqs = []
    for j in range(q_ref.shape[1] // HD):
        lanes = slice(j * HD, (j + 1) * HD)
        q_pair = halves_of(q_ref[:, lanes], half)
        do_pair = halves_of(do_ref[:, lanes], half)
        qr_pair = halves_of(qr_ref[:, lanes], half)
        qq = [jnp.concatenate([q_pair[i], qr_pair[i]], axis=1) for i in range(2)]
        p_aa, p_ba, p_bb = soft_parts(q_pair, k_pair, cols, rows_pos)
        g_aa = dot_nt(do_pair[0], v_pair[0])
        g_ba = dot_nt(do_pair[1], v_pair[0])
        g_bb = dot_nt(do_pair[1], v_pair[1])
        d_a = jnp.sum(p_aa * g_aa, axis=1, keepdims=True)
        d_b = jnp.sum(p_ba * g_ba, axis=1, keepdims=True) + jnp.sum(p_bb * g_bb, axis=1, keepdims=True)
        s_aa = (p_aa * (g_aa - d_a)).astype(BF)
        s_ba = (p_ba * (g_ba - d_b)).astype(BF)
        s_bb = (p_bb * (g_bb - d_b)).astype(BF)
        dq_pair = [dot(s_aa, kk[0]), dot(s_ba, kk[0]) + dot(s_bb, kk[1])]
        out = []
        for i in range(2):
            d = dq_pair[i] * scale
            out.append((d[:, :HD] * cos_pair[i] + d[:, HD:] * sin_pair[i]).astype(BF))
        dqs.append(merge_halves(out[0], out[1], half))
        acc_ref[0, :, : 2 * HD] += dot_tn(s_aa, qq[0]) + dot_tn(s_ba, qq[1])
        acc_ref[1, :, : 2 * HD] += dot_tn(s_bb, qq[1])
        acc_ref[0, :, 2 * HD : 3 * HD] += dot_tn(p_aa.astype(BF), do_pair[0]) + dot_tn(p_ba.astype(BF), do_pair[1])
        acc_ref[1, :, 2 * HD : 3 * HD] += dot_tn(p_bb.astype(BF), do_pair[1])
    dq_ref[...] = jnp.concatenate(dqs, axis=1)

    @pl.when(pl.program_id(0) == pl.num_programs(0) - 1)
    def _():
        dk = []
        for i in range(2):
            d = acc_ref[i, :, : 2 * HD] * scale
            dk.append((d[:, :HD] * cos_pair[i] + d[:, HD:] * sin_pair[i]).astype(BF))
        dk_ref[...] = merge_halves(dk[0], dk[1], half)
        dv_ref[...] = merge_halves(acc_ref[0, :, 2 * HD : 3 * HD].astype(BF), acc_ref[1, :, 2 * HD : 3 * HD].astype(BF), half)


def whole(shape):
    return pl.BlockSpec(shape, lambda g: (0,) * len(shape))


def attend(q, k, v, col, row, half):
    seq, q_cols = q.shape
    by_pair = pl.BlockSpec((seq, 2 * HD), lambda g: (0, g))
    return pl.pallas_call(
        functools.partial(attend_kernel, half),
        grid=(q_cols // (2 * HD),),
        in_specs=[by_pair, whole(k.shape), whole(v.shape), whole(col.shape), whole(row.shape)],
        out_specs=by_pair,
        out_shape=jax.ShapeDtypeStruct((seq, q_cols), BF),
        compiler_params=pltpu.CompilerParams(vmem_limit_bytes=56 * 2**20),
    )(q, k, v, col, row)


def attend_back(q, k, v, do, kr, qr, cos, sin, col, row, half):
    seq, q_cols = q.shape
    by_pair = pl.BlockSpec((seq, 2 * HD), lambda g: (0, g))
    return pl.pallas_call(
        functools.partial(attend_back_kernel, half),
        grid=(q_cols // (2 * HD),),
        in_specs=[by_pair, whole(k.shape), whole(v.shape), by_pair, whole(kr.shape), by_pair, whole(cos.shape), whole(sin.shape), whole(col.shape), whole(row.shape)],
        out_specs=[by_pair, whole(k.shape), whole(v.shape)],
        out_shape=[jax.ShapeDtypeStruct((seq, q_cols), BF), jax.ShapeDtypeStruct(k.shape, BF), jax.ShapeDtypeStruct(v.shape, BF)],
        scratch_shapes=[pltpu.VMEM((2, seq // 2, 4 * HD), F32)],
        compiler_params=pltpu.CompilerParams(vmem_limit_bytes=56 * 2**20),
    )(q, k, v, do, kr, qr, cos, sin, col, row)


def ffn_kernel(h_ref, g_ref, wgu_ref, wd_ref, z_ref, dgu_ref, out_ref, dh_ref):
    ff = z_ref.shape[1]
    gu = dot(h_ref[...], wgu_ref[...])
    gate, up = gu[:, :ff], gu[:, ff:]
    sig = 1.0 / (1.0 + jnp.exp(-gate))
    act = gate * sig
    z = (act * up).astype(BF)
    z_ref[...] = z
    dz = dot_nt(g_ref[...], wd_ref[...])
    dub = (dz * act).astype(BF)
    dgb = (dz * up * (sig * (1.0 + gate * (1.0 - sig)))).astype(BF)
    dgu = jnp.concatenate([dgb, dub], axis=1)
    dgu_ref[...] = dgu
    dh_ref[...] = dot_nt(dgu, wgu_ref[...]).astype(BF)
    out_ref[...] = dot(z, wd_ref[...]).astype(BF)


def ffn(h, g, w_gu, w_d, block):
    seq, width = h.shape
    ff = w_d.shape[0]
    rows = pl.BlockSpec((block, width), lambda i: (i, 0))
    return pl.pallas_call(
        ffn_kernel,
        grid=(seq // block,),
        in_specs=[rows, rows, whole(w_gu.shape), whole(w_d.shape)],
        out_specs=[pl.BlockSpec((block, ff), lambda i: (i, 0)), pl.BlockSpec((block, 2 * ff), lambda i: (i, 0)), rows, rows],
        out_shape=[jax.ShapeDtypeStruct((seq, ff), BF), jax.ShapeDtypeStruct((seq, 2 * ff), BF), jax.ShapeDtypeStruct((seq, width), BF), jax.ShapeDtypeStruct((seq, width), BF)],
        compiler_params=pltpu.CompilerParams(vmem_limit_bytes=56 * 2**20),
    )(h, g, w_gu, w_d)


def sum_kernel(*refs):
    total = refs[0][...].astype(F32)
    for ref in refs[1:-1]:
        total = total + ref[...].astype(F32)
    refs[-1][...] = total.astype(refs[-1].dtype)


def sum_pieces(pieces, cost):
    shape = pieces[0].shape
    block = pl.BlockSpec((1,) + shape[1:], lambda i: (i, 0, 0))
    return pl.pallas_call(
        sum_kernel,
        grid=(shape[0],),
        in_specs=[block] * len(pieces),
        out_specs=block,
        out_shape=jax.ShapeDtypeStruct(shape, BF),
        cost_estimate=pl.CostEstimate(flops=cost, bytes_accessed=cost // 300, transcendentals=0),
    )(*pieces)


def on_device(
    tokens,
    block_order,
    norm_attn,
    w_query,
    w_key,
    w_value,
    w_out,
    norm_ffn,
    w_gate,
    w_up,
    w_down,
    cotangent,
):
    c_count = lax.axis_size("ctx")
    f_count = lax.axis_size("fsdp")
    f_index = lax.axis_index("fsdp")
    tok_rows = tokens.shape[1]
    width = tokens.shape[2]
    seq = tok_rows * c_count
    half = tok_rows // 2
    heads = H // c_count
    share = c_count // KVH
    q_cols = heads * HD
    a_cols = q_cols + 2 * HD
    rows = w_query.shape[0]
    ff_cols = w_gate.shape[1] // c_count

    def to_dest(packed):
        return lax.all_to_all(packed, "ctx", split_axis=0, concat_axis=0, tiled=True)

    def by_dest(w):
        return w.reshape(rows, c_count, -1).transpose(1, 0, 2)

    def kv_dest(w):
        return jnp.repeat(w.reshape(rows, KVH, HD).transpose(1, 0, 2), share, axis=0)

    pos = positions(block_order, seq, tok_rows, c_count)
    cos_table, sin_table = rope_tables(pos)
    cos_wide = jnp.concatenate([cos_table, cos_table], axis=2)[:, 0]
    sin_wide = jnp.concatenate([sin_table, sin_table], axis=2)[:, 0]
    pos_col = pos[:, None]
    pos_row = pos.reshape(c_count, 2, half).transpose(1, 0, 2).reshape(2, seq // 2)
    x_all = gather_c(tokens[0])
    gain_pack = jnp.pad(jnp.stack([norm_attn, norm_ffn], axis=1), ((0, 0), (0, 126)))
    qkv_pack = jnp.concatenate(
        [
            by_dest(w_query),
            kv_dest(w_key),
            kv_dest(w_value),
            jnp.broadcast_to(gain_pack[None], (c_count, rows, 128)),
        ],
        axis=2,
    )
    moved_qkv = to_dest(qkv_pack)
    d_pieces = fetch_f(w_down, f_count)
    w_qkvg = place_f(fetch_f(after(moved_qkv, *d_pieces), f_count), 1, f_index).reshape(width, a_cols + 128)
    w_qkv = w_qkvg[:, :a_cols]
    unit = jnp.eye(8, 128, dtype=BF)
    gains = dot_nt(unit, w_qkvg[:, a_cols:])
    gain_a = gains[0]
    gain_f = gains[1]
    w_o = place_f(fetch_f(w_out, f_count), 0, f_index).reshape(f_count * rows, width)
    moved_gu = to_dest(after(jnp.concatenate([by_dest(w_gate), by_dest(w_up)], axis=2), moved_qkv))
    gu_pieces = fetch_f(moved_gu, f_count)

    x_seen = after(x_all, w_qkvg, w_o, moved_gu, cos_wide, sin_wide, pos_col, pos_row)
    normed_all, _ = rms_parts(x_seen.astype(F32))
    h1 = (normed_all * gain_a).astype(BF)
    g_all = gather_c(after(cotangent[0], h1))
    qkv = dot(h1, w_qkv)
    q = rotate(qkv[:, :q_cols].reshape(seq, heads, HD), cos_table, sin_table).astype(BF)
    k = rotate(qkv[:, None, q_cols : q_cols + HD], cos_table, sin_table).astype(BF)
    q_turn = turn(q).reshape(seq, q_cols)
    k_turn = turn(k)[:, 0]
    q = q.reshape(seq, q_cols)
    k = k[:, 0]
    v = qkv[:, q_cols + HD :].astype(BF)
    o = attend(q, k, v, pos_col, pos_row, half)
    y_part = dot(o, w_o).astype(BF)
    y_rows = scatter_c(after(y_part, g_all, q_turn, k_turn, *gu_pieces[:3]))

    source = tokens[0].astype(F32)
    residual = source + y_rows.astype(F32)
    normed_f, recip_f = rms_parts(residual)
    w_d = place_f(d_pieces, 0, f_index).reshape(ff_cols, width)
    w_gu = place_f(gu_pieces, 1, f_index).reshape(width, 2 * ff_cols)
    h2_rows = after((normed_f * gain_f).astype(BF), w_gu, w_d)
    h2 = gather_c(h2_rows)

    z, dgu, out_part, dh2_part = ffn(h2, g_all, w_gu, w_d, FFN_ROWS)
    dh2 = scatter_c(dh2_part)
    grad_gu_low = dot_tn(after(h2, dh2_part), dgu).astype(BF)
    sent_gu = send_f(grad_gu_low.reshape(c_count, f_count, rows, -1), 1, f_index, f_count)
    grad_down_low = dot_tn(z, after(g_all, grad_gu_low)).astype(BF)
    sent_down = send_f(grad_down_low.reshape(f_count, -1, width), 0, f_index, f_count)

    d_h = after(dh2, grad_down_low, *sent_gu[:3]).astype(F32)
    gain_terms_f = jnp.sum(d_h * normed_f, axis=0)
    d_res = cotangent[0].astype(F32) + norm_back(d_h * gain_f, normed_f, recip_f)
    ab_rows = d_res.astype(BF)
    ab = gather_c(ab_rows)
    sum_gu = sum_pieces([after(piece, ab_rows) for piece in sent_gu], SUM_COST)
    ab = after(ab, sum_gu)
    out_rows = scatter_c(after(out_part, ab))

    d_o = dot_nt(ab, w_o).astype(BF)
    owned_gu = to_dest(after(sum_gu, d_o))
    dq, dk, dv = attend_back(
        q, k, v, d_o, k_turn, q_turn, cos_wide, sin_wide, pos_col, pos_row, half
    )
    dqkv = jnp.concatenate([dq, dk, dv], axis=1)
    grad_qkv = dot_tn(h1, dqkv)
    gain_terms_a = jnp.sum(grad_qkv * w_qkv.astype(F32), axis=1) / gain_a
    terms = jnp.stack([gain_terms_a, gain_terms_f])
    high = terms.astype(BF)
    low = (terms - high.astype(F32)).astype(BF)
    gain_cols = dot_tn(jnp.concatenate([high, low]), jnp.eye(4, 128, dtype=BF)).astype(BF)
    grad_qkv_low = jnp.concatenate([grad_qkv.astype(BF), gain_cols], axis=1)
    sent_qkv = send_f(grad_qkv_low.reshape(c_count, f_count, rows, -1), 1, f_index, f_count)
    grad_out_low = dot_tn(after(o, grad_qkv_low), ab).astype(BF)
    sent_out = send_f(grad_out_low.reshape(f_count, rows, width), 0, f_index, f_count)
    dh1_cast = dot_nt(after(dqkv, grad_qkv_low), w_qkv).astype(BF)
    dh1_low = after(dh1_cast, owned_gu, out_rows, *sent_down, *sent_qkv)
    dh1 = scatter_c(dh1_low)
    sum_qkv = total_f(sent_qkv, dh1_low).astype(BF)
    shard_down = total_f(sent_down, sum_qkv)
    result = (residual + after(out_rows, sum_qkv).astype(F32)).astype(BF)
    owned_qkv = to_dest(sum_qkv)
    shard_out = total_f(sent_out)
    shard_gate = owned_gu[:, :, :ff_cols].transpose(1, 0, 2).reshape(rows, -1).astype(F32)
    shard_up = owned_gu[:, :, ff_cols:].transpose(1, 0, 2).reshape(rows, -1).astype(F32)
    shard_query = owned_qkv[:, :, :q_cols].transpose(1, 0, 2).reshape(rows, -1).astype(F32)
    grad_kv = jnp.sum(
        owned_qkv[:, :, q_cols:a_cols].reshape(KVH, share, rows, 2 * HD).astype(F32), axis=1
    )
    shard_key = grad_kv[:, :, :HD].transpose(1, 0, 2).reshape(rows, -1)
    shard_value = grad_kv[:, :, HD:].transpose(1, 0, 2).reshape(rows, -1)
    gain_sums = jnp.sum(owned_qkv[:, :, a_cols : a_cols + 4].astype(F32), axis=0)

    normed_a, recip_a = rms_parts(source)
    grads = d_res + norm_back(dh1.astype(F32) * gain_a, normed_a, recip_a)
    return (
        result[None],
        grads.astype(BF)[None],
        gain_sums[:, 0] + gain_sums[:, 2],
        shard_query,
        shard_key,
        shard_value,
        shard_out,
        gain_sums[:, 1] + gain_sums[:, 3],
        shard_gate,
        shard_up,
        shard_down,
    )


def solution(mesh):
    both = ("ctx", "fsdp")
    row = P(both, None)
    in_specs = (
        P("fsdp", "ctx", None),
        P(),
        P(both),
        row,
        row,
        row,
        row,
        P(both),
        row,
        row,
        row,
        P("fsdp", "ctx", None),
    )
    out_specs = (
        P("fsdp", "ctx", None),
        P("fsdp", "ctx", None),
        P(both),
        row,
        row,
        row,
        row,
        P(both),
        row,
        row,
        row,
    )
    return jax.shard_map(
        on_device, mesh=mesh, in_specs=in_specs, out_specs=out_specs, check_vma=False
    )
```

```python
import functools

import jax
import jax.numpy as jnp
from jax import lax
from jax.experimental import pallas as pl
from jax.experimental.pallas import tpu as pltpu
from jax.sharding import PartitionSpec as P

H = 32
KVH = 4
HD = 64

EPS = 1e-05
THETA = 10000.0
BF = jnp.bfloat16
F32 = jnp.float32
FFN_ROWS = 256


def rms_parts(values):
    recip = lax.rsqrt(jnp.mean(values * values, axis=-1, keepdims=True) + EPS)
    return (values * recip, recip)


def norm_back(grad_in, normed, recip):
    return recip * (grad_in - normed * jnp.mean(grad_in * normed, axis=-1, keepdims=True))


def positions(block_order, row_count, tok_rows, ctx_count):
    row_ids = jnp.arange(row_count, dtype=jnp.int32)
    owner_index = row_ids // tok_rows
    within = row_ids % tok_rows
    half_rows = tok_rows // 2
    match = owner_index[:, None] == jnp.arange(ctx_count, dtype=jnp.int32)[None, :]
    paired = jnp.sum(jnp.where(match, block_order[None, :], 0), axis=1)
    block_id = jnp.where(within < half_rows, paired, 2 * ctx_count - 1 - paired)
    return block_id * half_rows + within % half_rows


def rope_tables(pos):
    freqs = THETA ** (-(jnp.arange(HD // 2, dtype=F32) * 2.0 / HD))
    angles = pos.astype(F32)[:, None] * freqs[None, :]
    return (jnp.cos(angles)[:, None, :], jnp.sin(angles)[:, None, :])


def turn(values):
    return jnp.concatenate([values[..., HD // 2 :], -values[..., : HD // 2]], axis=-1)


def rotate(values, cos_table, sin_table):
    first_half = values[..., : HD // 2]
    second_half = values[..., HD // 2 :]
    return jnp.concatenate(
        [
            first_half * cos_table - second_half * sin_table,
            second_half * cos_table + first_half * sin_table,
        ],
        axis=-1,
    )


def after(value, *others):
    return lax.optimization_barrier((value,) + others)[0]


def swap_f(value, step, f_count):
    return lax.ppermute(value, "fsdp", [(i, i ^ step) for i in range(f_count)])


def swap_core(value, c_count):
    return lax.ppermute(value, "ctx", [(i, i ^ 1) for i in range(c_count)])


def pick(stack, index, axis=0):
    return lax.dynamic_index_in_dim(stack, index, axis, keepdims=False)


def place_f(pieces, axis, f_index):
    value = pieces[0]
    shape = value.shape[:axis] + (len(pieces),) + value.shape[axis:]
    out = jnp.zeros(shape, value.dtype)
    for step, piece in enumerate(pieces):
        out = lax.dynamic_update_index_in_dim(out, piece, f_index ^ step, axis)
    return out


def fetch_f(value, f_count):
    return [value] + [swap_f(value, step, f_count) for step in range(1, f_count)]


def send_f(parts, axis, f_index, f_count):
    pieces = []
    for step in range(f_count):
        piece = pick(parts, f_index ^ step, axis)
        pieces.append(swap_f(piece, step, f_count) if step else piece)
    return pieces


def total_f(pieces, *others):
    return sum(after(piece, *others).astype(F32) for piece in pieces)


def gather_c(rows):
    return lax.all_gather(rows, "ctx", axis=0, tiled=True)


def scatter_c(full):
    return lax.psum_scatter(full, "ctx", scatter_dimension=0, tiled=True)


def exchange_z(blocks, c_count):
    groups = [list(range(core, c_count, 2)) for core in range(2)]
    return lax.all_to_all(
        blocks, "ctx", split_axis=0, concat_axis=0, tiled=True, axis_index_groups=groups
    )


def pair_sum(full, c_count):
    core = lax.axis_index("ctx") % 2
    parts = full.reshape(c_count // 2, 2, full.shape[0] // c_count, full.shape[1])
    got = swap_core(pick(parts, 1 - core, 1), c_count)
    return (pick(parts, core, 1).astype(F32) + got.astype(F32)).astype(BF)


def dot(a, b):
    return jnp.dot(a, b, preferred_element_type=F32)


def dot_nt(a, b):
    return lax.dot_general(a, b, (((1,), (1,)), ((), ())), preferred_element_type=F32)


def dot_tn(a, b):
    return lax.dot_general(a, b, (((0,), (0,)), ((), ())), preferred_element_type=F32)


def halves_of(value, half):
    rows, cols = value.shape
    blocks = value.reshape(rows // (2 * half), 2, half, cols)
    return [blocks[:, i].reshape(rows // 2, cols) for i in range(2)]


def merge_halves(first, second, half):
    rows, cols = first.shape
    blocks = [v.reshape(rows // half, 1, half, cols) for v in (first, second)]
    return jnp.concatenate(blocks, axis=1).reshape(2 * rows, cols)


def soft_parts(q_pair, k_pair, cols, rows_pos):
    scale = HD ** (-0.5)
    s_aa = jnp.where(rows_pos[0] <= cols[0], dot_nt(q_pair[0], k_pair[0]) * scale, -jnp.inf)
    s_ba = dot_nt(q_pair[1], k_pair[0]) * scale
    s_bb = jnp.where(rows_pos[1] <= cols[1], dot_nt(q_pair[1], k_pair[1]) * scale, -jnp.inf)
    m_a = jnp.max(s_aa, axis=1, keepdims=True)
    m_b = jnp.maximum(jnp.max(s_ba, axis=1, keepdims=True), jnp.max(s_bb, axis=1, keepdims=True))
    e_aa, e_ba, e_bb = jnp.exp(s_aa - m_a), jnp.exp(s_ba - m_b), jnp.exp(s_bb - m_b)
    r_a = 1.0 / jnp.sum(e_aa, axis=1, keepdims=True)
    r_b = 1.0 / (jnp.sum(e_ba, axis=1, keepdims=True) + jnp.sum(e_bb, axis=1, keepdims=True))
    return e_aa * r_a, e_ba * r_b, e_bb * r_b


def attend_kernel(half, q_ref, k_ref, v_ref, col_ref, row_ref, o_ref):
    cols = halves_of(col_ref[...], half)
    rows_pos = [row_ref[0:1], row_ref[1:2]]
    k_pair, v_pair = halves_of(k_ref[...], half), halves_of(v_ref[...], half)
    outs = []
    for j in range(q_ref.shape[1] // HD):
        q_pair = halves_of(q_ref[:, j * HD : (j + 1) * HD], half)
        p_aa, p_ba, p_bb = soft_parts(q_pair, k_pair, cols, rows_pos)
        o_a = dot(p_aa.astype(BF), v_pair[0])
        o_b = dot(p_ba.astype(BF), v_pair[0]) + dot(p_bb.astype(BF), v_pair[1])
        outs.append(merge_halves(o_a.astype(BF), o_b.astype(BF), half))
    o_ref[...] = jnp.concatenate(outs, axis=1)


def attend_back_kernel(half, q_ref, k_ref, v_ref, do_ref, cos_ref, sin_ref, col_ref, row_ref, dq_ref, dk_ref, dv_ref, acc_ref):
    scale = HD ** (-0.5)
    cols = halves_of(col_ref[...], half)
    rows_pos = [row_ref[0:1], row_ref[1:2]]
    k_pair, v_pair = halves_of(k_ref[...], half), halves_of(v_ref[...], half)
    kk = [jnp.concatenate([k_pair[i], turn(k_pair[i])], axis=1) for i in range(2)]
    cos_pair, sin_pair = halves_of(cos_ref[...], half), halves_of(sin_ref[...], half)

    @pl.when(pl.program_id(0) == 0)
    def _():
        acc_ref[...] = jnp.zeros_like(acc_ref)

    dqs = []
    for j in range(q_ref.shape[1] // HD):
        lanes = slice(j * HD, (j + 1) * HD)
        q_pair = halves_of(q_ref[:, lanes], half)
        do_pair = halves_of(do_ref[:, lanes], half)
        qq = [jnp.concatenate([q_pair[i], turn(q_pair[i])], axis=1) for i in range(2)]
        p_aa, p_ba, p_bb = soft_parts(q_pair, k_pair, cols, rows_pos)
        g_aa = dot_nt(do_pair[0], v_pair[0])
        g_ba = dot_nt(do_pair[1], v_pair[0])
        g_bb = dot_nt(do_pair[1], v_pair[1])
        d_a = jnp.sum(p_aa * g_aa, axis=1, keepdims=True)
        d_b = jnp.sum(p_ba * g_ba, axis=1, keepdims=True) + jnp.sum(p_bb * g_bb, axis=1, keepdims=True)
        s_aa = (p_aa * (g_aa - d_a)).astype(BF)
        s_ba = (p_ba * (g_ba - d_b)).astype(BF)
        s_bb = (p_bb * (g_bb - d_b)).astype(BF)
        dq_pair = [dot(s_aa, kk[0]), dot(s_ba, kk[0]) + dot(s_bb, kk[1])]
        out = []
        for i in range(2):
            d = dq_pair[i] * scale
            out.append((d[:, :HD] * cos_pair[i] + d[:, HD:] * sin_pair[i]).astype(BF))
        dqs.append(merge_halves(out[0], out[1], half))
        acc_ref[0, :, : 2 * HD] += dot_tn(s_aa, qq[0]) + dot_tn(s_ba, qq[1])
        acc_ref[1, :, : 2 * HD] += dot_tn(s_bb, qq[1])
        acc_ref[0, :, 2 * HD : 3 * HD] += dot_tn(p_aa.astype(BF), do_pair[0]) + dot_tn(p_ba.astype(BF), do_pair[1])
        acc_ref[1, :, 2 * HD : 3 * HD] += dot_tn(p_bb.astype(BF), do_pair[1])
    dq_ref[...] = jnp.concatenate(dqs, axis=1)

    @pl.when(pl.program_id(0) == pl.num_programs(0) - 1)
    def _():
        dk = []
        for i in range(2):
            d = acc_ref[i, :, : 2 * HD] * scale
            dk.append((d[:, :HD] * cos_pair[i] + d[:, HD:] * sin_pair[i]).astype(BF))
        dk_ref[...] = merge_halves(dk[0], dk[1], half)
        dv_ref[...] = merge_halves(acc_ref[0, :, 2 * HD : 3 * HD].astype(BF), acc_ref[1, :, 2 * HD : 3 * HD].astype(BF), half)


def whole(shape):
    return pl.BlockSpec(shape, lambda g: (0,) * len(shape))


def attend(q, k, v, col, row, half):
    seq, q_cols = q.shape
    by_pair = pl.BlockSpec((seq, 2 * HD), lambda g: (0, g))
    return pl.pallas_call(
        functools.partial(attend_kernel, half),
        grid=(q_cols // (2 * HD),),
        in_specs=[by_pair, whole(k.shape), whole(v.shape), whole(col.shape), whole(row.shape)],
        out_specs=by_pair,
        out_shape=jax.ShapeDtypeStruct((seq, q_cols), BF),
        compiler_params=pltpu.CompilerParams(vmem_limit_bytes=56 * 2**20),
    )(q, k, v, col, row)


def attend_back(q, k, v, do, cos, sin, col, row, half):
    seq, q_cols = q.shape
    by_pair = pl.BlockSpec((seq, 2 * HD), lambda g: (0, g))
    return pl.pallas_call(
        functools.partial(attend_back_kernel, half),
        grid=(q_cols // (2 * HD),),
        in_specs=[by_pair, whole(k.shape), whole(v.shape), by_pair, whole(cos.shape), whole(sin.shape), whole(col.shape), whole(row.shape)],
        out_specs=[by_pair, whole(k.shape), whole(v.shape)],
        out_shape=[jax.ShapeDtypeStruct((seq, q_cols), BF), jax.ShapeDtypeStruct(k.shape, BF), jax.ShapeDtypeStruct(v.shape, BF)],
        scratch_shapes=[pltpu.VMEM((2, seq // 2, 4 * HD), F32)],
        compiler_params=pltpu.CompilerParams(vmem_limit_bytes=56 * 2**20),
    )(q, k, v, do, cos, sin, col, row)


def ffn_kernel(h_ref, g_ref, wgu_ref, wd_ref, z_ref, dgu_ref, out_ref, dh_ref):
    ff = z_ref.shape[1]
    gu = dot(h_ref[...], wgu_ref[...])
    gate, up = gu[:, :ff], gu[:, ff:]
    sig = 1.0 / (1.0 + jnp.exp(-gate))
    act = gate * sig
    z = (act * up).astype(BF)
    z_ref[...] = z
    dz = dot_nt(g_ref[...], wd_ref[...])
    dub = (dz * act).astype(BF)
    dgb = (dz * up * (sig * (1.0 + gate * (1.0 - sig)))).astype(BF)
    dgu = jnp.concatenate([dgb, dub], axis=1)
    dgu_ref[...] = dgu
    dh_ref[...] = dot_nt(dgu, wgu_ref[...]).astype(BF)
    out_ref[...] = dot(z, wd_ref[...]).astype(BF)


def ffn(h, g, w_gu, w_d, block):
    seq, width = h.shape
    ff = w_d.shape[0]
    rows = pl.BlockSpec((block, width), lambda i: (i, 0))
    return pl.pallas_call(
        ffn_kernel,
        grid=(seq // block,),
        in_specs=[rows, rows, whole(w_gu.shape), whole(w_d.shape)],
        out_specs=[pl.BlockSpec((block, ff), lambda i: (i, 0)), pl.BlockSpec((block, 2 * ff), lambda i: (i, 0)), rows, rows],
        out_shape=[jax.ShapeDtypeStruct((seq, ff), BF), jax.ShapeDtypeStruct((seq, 2 * ff), BF), jax.ShapeDtypeStruct((seq, width), BF), jax.ShapeDtypeStruct((seq, width), BF)],
        compiler_params=pltpu.CompilerParams(vmem_limit_bytes=56 * 2**20),
    )(h, g, w_gu, w_d)


def on_device(
    tokens,
    block_order,
    norm_attn,
    w_query,
    w_key,
    w_value,
    w_out,
    norm_ffn,
    w_gate,
    w_up,
    w_down,
    cotangent,
):
    c_count = lax.axis_size("ctx")
    f_count = lax.axis_size("fsdp")
    f_index = lax.axis_index("fsdp")
    tok_rows = tokens.shape[1]
    width = tokens.shape[2]
    seq = tok_rows * c_count
    half = tok_rows // 2
    heads = H // c_count
    share = c_count // KVH
    q_cols = heads * HD
    a_cols = q_cols + 2 * HD
    rows = w_query.shape[0]
    ff_cols = w_gate.shape[1] // c_count

    def to_dest(packed):
        return lax.all_to_all(packed, "ctx", split_axis=0, concat_axis=0, tiled=True)

    def by_dest(w):
        return w.reshape(rows, c_count, -1).transpose(1, 0, 2)

    def kv_dest(w):
        return jnp.repeat(w.reshape(rows, KVH, HD).transpose(1, 0, 2), share, axis=0)

    pos = positions(block_order, seq, tok_rows, c_count)
    cos_table, sin_table = rope_tables(pos)
    cos_wide = jnp.concatenate([cos_table, cos_table], axis=2)[:, 0]
    sin_wide = jnp.concatenate([sin_table, sin_table], axis=2)[:, 0]
    pos_col = pos[:, None]
    pos_row = pos.reshape(c_count, 2, half).transpose(1, 0, 2).reshape(2, seq // 2)
    x_all = gather_c(tokens[0])
    gain_pack = jnp.pad(jnp.stack([norm_attn, norm_ffn], axis=1), ((0, 0), (0, 126)))
    qkv_pack = jnp.concatenate(
        [
            by_dest(w_query),
            kv_dest(w_key),
            kv_dest(w_value),
            jnp.broadcast_to(gain_pack[None], (c_count, rows, 128)),
        ],
        axis=2,
    )
    moved_qkv = to_dest(qkv_pack)
    d_pieces = fetch_f(w_down, f_count)
    w_qkvg = place_f(fetch_f(after(moved_qkv, *d_pieces), f_count), 1, f_index).reshape(width, a_cols + 128)
    w_qkv = w_qkvg[:, :a_cols]
    unit = jnp.eye(8, 128, dtype=BF)
    gains = dot_nt(unit, w_qkvg[:, a_cols:])
    gain_a = gains[0]
    gain_f = gains[1]
    w_o = place_f(fetch_f(w_out, f_count), 0, f_index).reshape(f_count * rows, width)
    moved_gu = to_dest(after(jnp.concatenate([by_dest(w_gate), by_dest(w_up)], axis=2), moved_qkv))
    gu_pieces = fetch_f(moved_gu, f_count)

    x_seen = after(x_all, w_qkvg, w_o, moved_gu, cos_wide, sin_wide, pos_col, pos_row)
    g_all = gather_c(after(cotangent[0], x_seen))
    normed_all, _ = rms_parts(x_seen.astype(F32))
    h1 = (normed_all * gain_a).astype(BF)
    qkv = dot(h1, w_qkv)
    q = rotate(qkv[:, :q_cols].reshape(seq, heads, HD), cos_table, sin_table).astype(BF)
    k = rotate(qkv[:, None, q_cols : q_cols + HD], cos_table, sin_table).astype(BF)
    q = q.reshape(seq, q_cols)
    k = k[:, 0]
    v = qkv[:, q_cols + HD :].astype(BF)
    o = attend(q, k, v, pos_col, pos_row, half)
    y_part = dot(o, w_o).astype(BF)
    y_rows = scatter_c(after(y_part, g_all, *gu_pieces[:3]))

    source = tokens[0].astype(F32)
    residual = source + y_rows.astype(F32)
    normed_f, recip_f = rms_parts(residual)
    w_d = place_f(d_pieces, 0, f_index).reshape(ff_cols, width)
    w_gu = place_f(gu_pieces, 1, f_index).reshape(width, 2 * ff_cols)
    h2_rows = after((normed_f * gain_f).astype(BF), w_gu, w_d)
    h2 = gather_c(h2_rows)

    z, dgu, out_part, dh2_part = ffn(h2, g_all, w_gu, w_d, FFN_ROWS)
    dh2 = scatter_c(dh2_part)
    grad_gu_low = dot_tn(after(h2, dh2_part), dgu).astype(BF)
    sent_gu = send_f(grad_gu_low.reshape(c_count, f_count, rows, -1), 1, f_index, f_count)
    grad_down_low = dot_tn(z, after(g_all, grad_gu_low)).astype(BF)
    sent_down = send_f(grad_down_low.reshape(f_count, -1, width), 0, f_index, f_count)

    d_h = after(dh2, grad_down_low, *sent_gu[:3]).astype(F32)
    gain_terms_f = jnp.sum(d_h * normed_f, axis=0)
    d_res = cotangent[0].astype(F32) + norm_back(d_h * gain_f, normed_f, recip_f)
    ab_rows = d_res.astype(BF)
    ab = gather_c(ab_rows)
    sum_gu = total_f(sent_gu, ab_rows).astype(BF)
    ab = after(ab, sum_gu)
    out_rows = scatter_c(after(out_part, ab))

    d_o = dot_nt(ab, w_o).astype(BF)
    owned_gu = to_dest(after(sum_gu, d_o))
    dq, dk, dv = attend_back(
        q, k, v, d_o, cos_wide, sin_wide, pos_col, pos_row, half
    )
    dqkv = jnp.concatenate([dq, dk, dv], axis=1)
    grad_qkv = dot_tn(h1, dqkv)
    gain_terms_a = jnp.sum(grad_qkv * w_qkv.astype(F32), axis=1) / gain_a
    terms = jnp.stack([gain_terms_a, gain_terms_f])
    high = terms.astype(BF)
    low = (terms - high.astype(F32)).astype(BF)
    gain_cols = dot_tn(jnp.concatenate([high, low]), jnp.eye(4, 128, dtype=BF)).astype(BF)
    grad_qkv_low = jnp.concatenate([grad_qkv.astype(BF), gain_cols], axis=1)
    sent_qkv = send_f(grad_qkv_low.reshape(c_count, f_count, rows, -1), 1, f_index, f_count)
    grad_out_low = dot_tn(after(o, grad_qkv_low), ab).astype(BF)
    sent_out = send_f(grad_out_low.reshape(f_count, rows, width), 0, f_index, f_count)
    dh1_cast = dot_nt(after(dqkv, grad_qkv_low), w_qkv).astype(BF)
    dh1_low = after(dh1_cast, owned_gu, out_rows, *sent_down, *sent_qkv)
    dh1 = scatter_c(dh1_low)
    sum_qkv = total_f(sent_qkv, dh1_low).astype(BF)
    shard_down = total_f(sent_down, sum_qkv)
    result = (residual + after(out_rows, sum_qkv).astype(F32)).astype(BF)
    owned_qkv = to_dest(sum_qkv)
    shard_out = total_f(sent_out)
    shard_gate = owned_gu[:, :, :ff_cols].transpose(1, 0, 2).reshape(rows, -1).astype(F32)
    shard_up = owned_gu[:, :, ff_cols:].transpose(1, 0, 2).reshape(rows, -1).astype(F32)
    shard_query = owned_qkv[:, :, :q_cols].transpose(1, 0, 2).reshape(rows, -1).astype(F32)
    grad_kv = jnp.sum(
        owned_qkv[:, :, q_cols:a_cols].reshape(KVH, share, rows, 2 * HD).astype(F32), axis=1
    )
    shard_key = grad_kv[:, :, :HD].transpose(1, 0, 2).reshape(rows, -1)
    shard_value = grad_kv[:, :, HD:].transpose(1, 0, 2).reshape(rows, -1)
    gain_sums = jnp.sum(owned_qkv[:, :, a_cols : a_cols + 4].astype(F32), axis=0)

    normed_a, recip_a = rms_parts(source)
    grads = d_res + norm_back(dh1.astype(F32) * gain_a, normed_a, recip_a)
    return (
        result[None],
        grads.astype(BF)[None],
        gain_sums[:, 0] + gain_sums[:, 2],
        shard_query,
        shard_key,
        shard_value,
        shard_out,
        gain_sums[:, 1] + gain_sums[:, 3],
        shard_gate,
        shard_up,
        shard_down,
    )


def solution(mesh):
    both = ("ctx", "fsdp")
    row = P(both, None)
    in_specs = (
        P("fsdp", "ctx", None),
        P(),
        P(both),
        row,
        row,
        row,
        row,
        P(both),
        row,
        row,
        row,
        P("fsdp", "ctx", None),
    )
    out_specs = (
        P("fsdp", "ctx", None),
        P("fsdp", "ctx", None),
        P(both),
        row,
        row,
        row,
        row,
        P(both),
        row,
        row,
        row,
    )
    return jax.shard_map(
        on_device, mesh=mesh, in_specs=in_specs, out_specs=out_specs, check_vma=False
    )
```

```python
import functools

import jax
import jax.numpy as jnp
from jax import lax
from jax.experimental import pallas as pl
from jax.experimental.pallas import tpu as pltpu
from jax.sharding import PartitionSpec as P

H = 32
KVH = 4
HD = 64

EPS = 1e-05
THETA = 10000.0
BF = jnp.bfloat16
F32 = jnp.float32
FFN_ROWS = 256


def rms_parts(values):
    recip = lax.rsqrt(jnp.mean(values * values, axis=-1, keepdims=True) + EPS)
    return (values * recip, recip)


def norm_back(grad_in, normed, recip):
    return recip * (grad_in - normed * jnp.mean(grad_in * normed, axis=-1, keepdims=True))


def positions(block_order, row_count, tok_rows, ctx_count):
    row_ids = jnp.arange(row_count, dtype=jnp.int32)
    owner_index = row_ids // tok_rows
    within = row_ids % tok_rows
    half_rows = tok_rows // 2
    match = owner_index[:, None] == jnp.arange(ctx_count, dtype=jnp.int32)[None, :]
    paired = jnp.sum(jnp.where(match, block_order[None, :], 0), axis=1)
    block_id = jnp.where(within < half_rows, paired, 2 * ctx_count - 1 - paired)
    return block_id * half_rows + within % half_rows


def rope_tables(pos):
    freqs = THETA ** (-(jnp.arange(HD // 2, dtype=F32) * 2.0 / HD))
    angles = pos.astype(F32)[:, None] * freqs[None, :]
    return (jnp.cos(angles)[:, None, :], jnp.sin(angles)[:, None, :])


def turn(values):
    return jnp.concatenate([values[..., HD // 2 :], -values[..., : HD // 2]], axis=-1)


def rotate(values, cos_table, sin_table):
    first_half = values[..., : HD // 2]
    second_half = values[..., HD // 2 :]
    return jnp.concatenate(
        [
            first_half * cos_table - second_half * sin_table,
            second_half * cos_table + first_half * sin_table,
        ],
        axis=-1,
    )


def after(value, *others):
    return lax.optimization_barrier((value,) + others)[0]


def swap_f(value, step, f_count):
    return lax.ppermute(value, "fsdp", [(i, i ^ step) for i in range(f_count)])


def swap_core(value, c_count):
    return lax.ppermute(value, "ctx", [(i, i ^ 1) for i in range(c_count)])


def pick(stack, index, axis=0):
    return lax.dynamic_index_in_dim(stack, index, axis, keepdims=False)


def place_f(pieces, axis, f_index):
    value = pieces[0]
    shape = value.shape[:axis] + (len(pieces),) + value.shape[axis:]
    out = jnp.zeros(shape, value.dtype)
    for step, piece in enumerate(pieces):
        out = lax.dynamic_update_index_in_dim(out, piece, f_index ^ step, axis)
    return out


def fetch_f(value, f_count):
    return [value] + [swap_f(value, step, f_count) for step in range(1, f_count)]


def send_f(parts, axis, f_index, f_count):
    pieces = []
    for step in range(f_count):
        piece = pick(parts, f_index ^ step, axis)
        pieces.append(swap_f(piece, step, f_count) if step else piece)
    return pieces


def total_f(pieces, *others):
    return sum(after(piece, *others).astype(F32) for piece in pieces)


def gather_c(rows):
    return lax.all_gather(rows, "ctx", axis=0, tiled=True)


def scatter_c(full):
    return lax.psum_scatter(full, "ctx", scatter_dimension=0, tiled=True)


def exchange_z(blocks, c_count):
    groups = [list(range(core, c_count, 2)) for core in range(2)]
    return lax.all_to_all(
        blocks, "ctx", split_axis=0, concat_axis=0, tiled=True, axis_index_groups=groups
    )


def pair_sum(full, c_count):
    core = lax.axis_index("ctx") % 2
    parts = full.reshape(c_count // 2, 2, full.shape[0] // c_count, full.shape[1])
    got = swap_core(pick(parts, 1 - core, 1), c_count)
    return (pick(parts, core, 1).astype(F32) + got.astype(F32)).astype(BF)


def dot(a, b):
    return jnp.dot(a, b, preferred_element_type=F32)


def dot_nt(a, b):
    return lax.dot_general(a, b, (((1,), (1,)), ((), ())), preferred_element_type=F32)


def dot_tn(a, b):
    return lax.dot_general(a, b, (((0,), (0,)), ((), ())), preferred_element_type=F32)


def halves_of(value, half):
    rows, cols = value.shape
    blocks = value.reshape(rows // (2 * half), 2, half, cols)
    return [blocks[:, i].reshape(rows // 2, cols) for i in range(2)]


def merge_halves(first, second, half):
    rows, cols = first.shape
    blocks = [v.reshape(rows // half, 1, half, cols) for v in (first, second)]
    return jnp.concatenate(blocks, axis=1).reshape(2 * rows, cols)


def soft_parts(q_pair, k_pair, cols, rows_pos):
    scale = HD ** (-0.5)
    s_aa = jnp.where(rows_pos[0] <= cols[0], dot_nt(q_pair[0], k_pair[0]) * scale, -jnp.inf)
    s_ba = dot_nt(q_pair[1], k_pair[0]) * scale
    s_bb = jnp.where(rows_pos[1] <= cols[1], dot_nt(q_pair[1], k_pair[1]) * scale, -jnp.inf)
    m_a = jnp.max(s_aa, axis=1, keepdims=True)
    m_b = jnp.maximum(jnp.max(s_ba, axis=1, keepdims=True), jnp.max(s_bb, axis=1, keepdims=True))
    e_aa, e_ba, e_bb = jnp.exp(s_aa - m_a), jnp.exp(s_ba - m_b), jnp.exp(s_bb - m_b)
    r_a = 1.0 / jnp.sum(e_aa, axis=1, keepdims=True)
    r_b = 1.0 / (jnp.sum(e_ba, axis=1, keepdims=True) + jnp.sum(e_bb, axis=1, keepdims=True))
    return e_aa * r_a, e_ba * r_b, e_bb * r_b


def attend_kernel(half, q_ref, k_ref, v_ref, col_ref, row_ref, o_ref):
    cols = halves_of(col_ref[...], half)
    rows_pos = [row_ref[0:1], row_ref[1:2]]
    k_pair, v_pair = halves_of(k_ref[...], half), halves_of(v_ref[...], half)
    outs = []
    for j in range(q_ref.shape[1] // HD):
        q_pair = halves_of(q_ref[:, j * HD : (j + 1) * HD], half)
        p_aa, p_ba, p_bb = soft_parts(q_pair, k_pair, cols, rows_pos)
        o_a = dot(p_aa.astype(BF), v_pair[0])
        o_b = dot(p_ba.astype(BF), v_pair[0]) + dot(p_bb.astype(BF), v_pair[1])
        outs.append(merge_halves(o_a.astype(BF), o_b.astype(BF), half))
    o_ref[...] = jnp.concatenate(outs, axis=1)


def attend_back_kernel(half, q_ref, k_ref, v_ref, do_ref, cos_ref, sin_ref, col_ref, row_ref, dq_ref, dk_ref, dv_ref, acc_ref):
    scale = HD ** (-0.5)
    cols = halves_of(col_ref[...], half)
    rows_pos = [row_ref[0:1], row_ref[1:2]]
    k_pair, v_pair = halves_of(k_ref[...], half), halves_of(v_ref[...], half)
    kk = [jnp.concatenate([k_pair[i], turn(k_pair[i])], axis=1) for i in range(2)]
    cos_pair, sin_pair = halves_of(cos_ref[...], half), halves_of(sin_ref[...], half)

    @pl.when(pl.program_id(0) == 0)
    def _():
        acc_ref[...] = jnp.zeros_like(acc_ref)

    dqs = []
    for j in range(q_ref.shape[1] // HD):
        lanes = slice(j * HD, (j + 1) * HD)
        q_pair = halves_of(q_ref[:, lanes], half)
        do_pair = halves_of(do_ref[:, lanes], half)
        qq = [jnp.concatenate([q_pair[i], turn(q_pair[i])], axis=1) for i in range(2)]
        p_aa, p_ba, p_bb = soft_parts(q_pair, k_pair, cols, rows_pos)
        g_aa = dot_nt(do_pair[0], v_pair[0])
        g_ba = dot_nt(do_pair[1], v_pair[0])
        g_bb = dot_nt(do_pair[1], v_pair[1])
        d_a = jnp.sum(p_aa * g_aa, axis=1, keepdims=True)
        d_b = jnp.sum(p_ba * g_ba, axis=1, keepdims=True) + jnp.sum(p_bb * g_bb, axis=1, keepdims=True)
        s_aa = (p_aa * (g_aa - d_a)).astype(BF)
        s_ba = (p_ba * (g_ba - d_b)).astype(BF)
        s_bb = (p_bb * (g_bb - d_b)).astype(BF)
        dq_pair = [dot(s_aa, kk[0]), dot(s_ba, kk[0]) + dot(s_bb, kk[1])]
        out = []
        for i in range(2):
            d = dq_pair[i] * scale
            out.append((d[:, :HD] * cos_pair[i] + d[:, HD:] * sin_pair[i]).astype(BF))
        dqs.append(merge_halves(out[0], out[1], half))
        acc_ref[0, :, : 2 * HD] += dot_tn(s_aa, qq[0]) + dot_tn(s_ba, qq[1])
        acc_ref[1, :, : 2 * HD] += dot_tn(s_bb, qq[1])
        acc_ref[0, :, 2 * HD : 3 * HD] += dot_tn(p_aa.astype(BF), do_pair[0]) + dot_tn(p_ba.astype(BF), do_pair[1])
        acc_ref[1, :, 2 * HD : 3 * HD] += dot_tn(p_bb.astype(BF), do_pair[1])
    dq_ref[...] = jnp.concatenate(dqs, axis=1)

    @pl.when(pl.program_id(0) == pl.num_programs(0) - 1)
    def _():
        dk = []
        for i in range(2):
            d = acc_ref[i, :, : 2 * HD] * scale
            dk.append((d[:, :HD] * cos_pair[i] + d[:, HD:] * sin_pair[i]).astype(BF))
        dk_ref[...] = merge_halves(dk[0], dk[1], half)
        dv_ref[...] = merge_halves(acc_ref[0, :, 2 * HD : 3 * HD].astype(BF), acc_ref[1, :, 2 * HD : 3 * HD].astype(BF), half)


def whole(shape):
    return pl.BlockSpec(shape, lambda g: (0,) * len(shape))


def attend(q, k, v, col, row, half):
    seq, q_cols = q.shape
    by_pair = pl.BlockSpec((seq, 2 * HD), lambda g: (0, g))
    return pl.pallas_call(
        functools.partial(attend_kernel, half),
        grid=(q_cols // (2 * HD),),
        in_specs=[by_pair, whole(k.shape), whole(v.shape), whole(col.shape), whole(row.shape)],
        out_specs=by_pair,
        out_shape=jax.ShapeDtypeStruct((seq, q_cols), BF),
        compiler_params=pltpu.CompilerParams(vmem_limit_bytes=56 * 2**20),
    )(q, k, v, col, row)


def attend_back(q, k, v, do, cos, sin, col, row, half):
    seq, q_cols = q.shape
    by_pair = pl.BlockSpec((seq, 2 * HD), lambda g: (0, g))
    return pl.pallas_call(
        functools.partial(attend_back_kernel, half),
        grid=(q_cols // (2 * HD),),
        in_specs=[by_pair, whole(k.shape), whole(v.shape), by_pair, whole(cos.shape), whole(sin.shape), whole(col.shape), whole(row.shape)],
        out_specs=[by_pair, whole(k.shape), whole(v.shape)],
        out_shape=[jax.ShapeDtypeStruct((seq, q_cols), BF), jax.ShapeDtypeStruct(k.shape, BF), jax.ShapeDtypeStruct(v.shape, BF)],
        scratch_shapes=[pltpu.VMEM((2, seq // 2, 4 * HD), F32)],
        compiler_params=pltpu.CompilerParams(vmem_limit_bytes=56 * 2**20),
    )(q, k, v, do, cos, sin, col, row)


def ffn_kernel(h_ref, g_ref, wgu_ref, wd_ref, z_ref, dgu_ref, dh_ref):
    ff = z_ref.shape[1]
    gu = dot(h_ref[...], wgu_ref[...])
    gate, up = gu[:, :ff], gu[:, ff:]
    sig = 1.0 / (1.0 + jnp.exp(-gate))
    act = gate * sig
    z = (act * up).astype(BF)
    z_ref[...] = z
    dz = dot_nt(g_ref[...], wd_ref[...])
    dub = (dz * act).astype(BF)
    dgb = (dz * up * (sig * (1.0 + gate * (1.0 - sig)))).astype(BF)
    dgu = jnp.concatenate([dgb, dub], axis=1)
    dgu_ref[...] = dgu
    dh_ref[...] = dot_nt(dgu, wgu_ref[...]).astype(BF)


def ffn(h, g, w_gu, w_d, block):
    seq, width = h.shape
    ff = w_d.shape[0]
    rows = pl.BlockSpec((block, width), lambda i: (i, 0))
    return pl.pallas_call(
        ffn_kernel,
        grid=(seq // block,),
        in_specs=[rows, rows, whole(w_gu.shape), whole(w_d.shape)],
        out_specs=[pl.BlockSpec((block, ff), lambda i: (i, 0)), pl.BlockSpec((block, 2 * ff), lambda i: (i, 0)), rows],
        out_shape=[jax.ShapeDtypeStruct((seq, ff), BF), jax.ShapeDtypeStruct((seq, 2 * ff), BF), jax.ShapeDtypeStruct((seq, width), BF)],
        compiler_params=pltpu.CompilerParams(vmem_limit_bytes=56 * 2**20),
    )(h, g, w_gu, w_d)


def on_device(
    tokens,
    block_order,
    norm_attn,
    w_query,
    w_key,
    w_value,
    w_out,
    norm_ffn,
    w_gate,
    w_up,
    w_down,
    cotangent,
):
    c_count = lax.axis_size("ctx")
    f_count = lax.axis_size("fsdp")
    f_index = lax.axis_index("fsdp")
    tok_rows = tokens.shape[1]
    width = tokens.shape[2]
    seq = tok_rows * c_count
    half = tok_rows // 2
    heads = H // c_count
    share = c_count // KVH
    q_cols = heads * HD
    a_cols = q_cols + 2 * HD
    rows = w_query.shape[0]
    ff_cols = w_gate.shape[1] // c_count

    def to_dest(packed):
        return lax.all_to_all(packed, "ctx", split_axis=0, concat_axis=0, tiled=True)

    def by_dest(w):
        return w.reshape(rows, c_count, -1).transpose(1, 0, 2)

    def kv_dest(w):
        return jnp.repeat(w.reshape(rows, KVH, HD).transpose(1, 0, 2), share, axis=0)

    pos = positions(block_order, seq, tok_rows, c_count)
    cos_table, sin_table = rope_tables(pos)
    cos_wide = jnp.concatenate([cos_table, cos_table], axis=2)[:, 0]
    sin_wide = jnp.concatenate([sin_table, sin_table], axis=2)[:, 0]
    pos_col = pos[:, None]
    pos_row = pos.reshape(c_count, 2, half).transpose(1, 0, 2).reshape(2, seq // 2)
    x_all = gather_c(tokens[0])
    gain_pack = jnp.pad(jnp.stack([norm_attn, norm_ffn], axis=1), ((0, 0), (0, 126)))
    qkv_pack = jnp.concatenate(
        [
            by_dest(w_query),
            kv_dest(w_key),
            kv_dest(w_value),
            jnp.broadcast_to(gain_pack[None], (c_count, rows, 128)),
        ],
        axis=2,
    )
    moved_qkv = to_dest(qkv_pack)
    d_pieces = fetch_f(w_down, f_count)
    w_qkvg = place_f(fetch_f(after(moved_qkv, *d_pieces), f_count), 1, f_index).reshape(width, a_cols + 128)
    w_qkv = w_qkvg[:, :a_cols]
    unit = jnp.eye(8, 128, dtype=BF)
    gains = dot_nt(unit, w_qkvg[:, a_cols:])
    gain_a = gains[0]
    gain_f = gains[1]
    w_o = place_f(fetch_f(w_out, f_count), 0, f_index).reshape(f_count * rows, width)
    moved_gu = to_dest(after(jnp.concatenate([by_dest(w_gate), by_dest(w_up)], axis=2), moved_qkv))
    gu_pieces = fetch_f(moved_gu, f_count)

    x_seen = after(x_all, w_qkvg, w_o, moved_gu, cos_wide, sin_wide, pos_col, pos_row)
    g_all = gather_c(after(cotangent[0], x_seen))
    normed_all, _ = rms_parts(x_seen.astype(F32))
    h1 = (normed_all * gain_a).astype(BF)
    qkv = dot(h1, w_qkv)
    q = rotate(qkv[:, :q_cols].reshape(seq, heads, HD), cos_table, sin_table).astype(BF)
    k = rotate(qkv[:, None, q_cols : q_cols + HD], cos_table, sin_table).astype(BF)
    q = q.reshape(seq, q_cols)
    k = k[:, 0]
    v = qkv[:, q_cols + HD :].astype(BF)
    o = attend(q, k, v, pos_col, pos_row, half)
    y_part = dot(o, w_o).astype(BF)
    y_rows = scatter_c(after(y_part, g_all, *gu_pieces[:3]))

    source = tokens[0].astype(F32)
    residual = source + y_rows.astype(F32)
    normed_f, recip_f = rms_parts(residual)
    w_d = place_f(d_pieces, 0, f_index).reshape(ff_cols, width)
    w_gu = place_f(gu_pieces, 1, f_index).reshape(width, 2 * ff_cols)
    h2_rows = after((normed_f * gain_f).astype(BF), w_gu, w_d)
    h2 = gather_c(h2_rows)

    z, dgu, dh2_part = ffn(h2, g_all, w_gu, w_d, FFN_ROWS)
    dh2 = scatter_c(dh2_part)
    grad_gu_low = dot_tn(after(h2, dh2_part), dgu).astype(BF)
    sent_gu = send_f(grad_gu_low.reshape(c_count, f_count, rows, -1), 1, f_index, f_count)
    grad_down_low = dot_tn(z, after(g_all, grad_gu_low)).astype(BF)
    sent_down = send_f(grad_down_low.reshape(f_count, -1, width), 0, f_index, f_count)

    out_part = dot(after(z, grad_down_low), w_d).astype(BF)
    d_h = after(dh2, out_part, *sent_gu[:3]).astype(F32)
    gain_terms_f = jnp.sum(d_h * normed_f, axis=0)
    d_res = cotangent[0].astype(F32) + norm_back(d_h * gain_f, normed_f, recip_f)
    ab_rows = d_res.astype(BF)
    ab = gather_c(ab_rows)
    sum_gu = total_f(sent_gu, ab_rows).astype(BF)
    ab = after(ab, sum_gu)
    out_rows = scatter_c(after(out_part, ab))

    d_o = dot_nt(ab, w_o).astype(BF)
    owned_gu = to_dest(after(sum_gu, d_o))
    dq, dk, dv = attend_back(
        q, k, v, d_o, cos_wide, sin_wide, pos_col, pos_row, half
    )
    dqkv = jnp.concatenate([dq, dk, dv], axis=1)
    grad_qkv = dot_tn(h1, dqkv)
    gain_terms_a = jnp.sum(grad_qkv * w_qkv.astype(F32), axis=1) / gain_a
    terms = jnp.stack([gain_terms_a, gain_terms_f])
    high = terms.astype(BF)
    low = (terms - high.astype(F32)).astype(BF)
    gain_cols = dot_tn(jnp.concatenate([high, low]), jnp.eye(4, 128, dtype=BF)).astype(BF)
    grad_qkv_low = jnp.concatenate([grad_qkv.astype(BF), gain_cols], axis=1)
    sent_qkv = send_f(grad_qkv_low.reshape(c_count, f_count, rows, -1), 1, f_index, f_count)
    grad_out_low = dot_tn(after(o, grad_qkv_low), ab).astype(BF)
    sent_out = send_f(grad_out_low.reshape(f_count, rows, width), 0, f_index, f_count)
    dh1_cast = dot_nt(after(dqkv, grad_qkv_low), w_qkv).astype(BF)
    dh1_low = after(dh1_cast, owned_gu, out_rows, *sent_down, *sent_qkv)
    dh1 = scatter_c(dh1_low)
    sum_qkv = total_f(sent_qkv, dh1_low).astype(BF)
    shard_down = total_f(sent_down, sum_qkv)
    result = (residual + after(out_rows, sum_qkv).astype(F32)).astype(BF)
    owned_qkv = to_dest(sum_qkv)
    shard_out = total_f(sent_out)
    shard_gate = owned_gu[:, :, :ff_cols].transpose(1, 0, 2).reshape(rows, -1).astype(F32)
    shard_up = owned_gu[:, :, ff_cols:].transpose(1, 0, 2).reshape(rows, -1).astype(F32)
    shard_query = owned_qkv[:, :, :q_cols].transpose(1, 0, 2).reshape(rows, -1).astype(F32)
    grad_kv = jnp.sum(
        owned_qkv[:, :, q_cols:a_cols].reshape(KVH, share, rows, 2 * HD).astype(F32), axis=1
    )
    shard_key = grad_kv[:, :, :HD].transpose(1, 0, 2).reshape(rows, -1)
    shard_value = grad_kv[:, :, HD:].transpose(1, 0, 2).reshape(rows, -1)
    gain_sums = jnp.sum(owned_qkv[:, :, a_cols : a_cols + 4].astype(F32), axis=0)

    normed_a, recip_a = rms_parts(source)
    grads = d_res + norm_back(dh1.astype(F32) * gain_a, normed_a, recip_a)
    return (
        result[None],
        grads.astype(BF)[None],
        gain_sums[:, 0] + gain_sums[:, 2],
        shard_query,
        shard_key,
        shard_value,
        shard_out,
        gain_sums[:, 1] + gain_sums[:, 3],
        shard_gate,
        shard_up,
        shard_down,
    )


def solution(mesh):
    both = ("ctx", "fsdp")
    row = P(both, None)
    in_specs = (
        P("fsdp", "ctx", None),
        P(),
        P(both),
        row,
        row,
        row,
        row,
        P(both),
        row,
        row,
        row,
        P("fsdp", "ctx", None),
    )
    out_specs = (
        P("fsdp", "ctx", None),
        P("fsdp", "ctx", None),
        P(both),
        row,
        row,
        row,
        row,
        P(both),
        row,
        row,
        row,
    )
    return jax.shard_map(
        on_device, mesh=mesh, in_specs=in_specs, out_specs=out_specs, check_vma=False
    )
```
